512 devices in a mesh: tile: 64 (over z_lo, y, core), fsdp: 8 (over x, z_hi).
Axes of the slice: x: 4, y: 4, z: 16 (z_hi: 2, z_lo: 8; z = z_hi * 8 + z_lo), core: 2. Of those that a mesh axis runs over, the one named last changes fastest.
Arguments:
- tokens: bfloat16 [8, 64, 16, 16, 1024], P('fsdp', 'tile'), may hold values from -6 to 6
- w_qkv: bfloat16 [1024, 1536], P('fsdp')
- w_out: bfloat16 [512, 1024], P('fsdp'), may hold values from -0.25 to 0.25
- rel_bias: float32 [8, 15, 15], replicated, may hold values from -4 to 4
- seam_codes: int32 [64, 3], P('tile'), may hold values from 0 to 3
- corner_open: int32 [64], P('tile'), may hold values from 0 to 1, as said below
- grad_out: bfloat16 [8, 64, 16, 16, 1024], P('fsdp', 'tile'), may hold values from -6 to 6
Outputs:
- output: bfloat16 [8, 64, 16, 16, 1024], P('fsdp', 'tile')
- grad_tokens: bfloat16 [8, 64, 16, 16, 1024], P('fsdp', 'tile')
- grad_w_qkv: float32 [1024, 1536], P('fsdp', 'tile')
- grad_w_out: float32 [512, 1024], P('fsdp', 'tile')
The draws below stay inside these ranges and needn't reach their ends.
Inputs may be any that keep to these rules, and one draw needn't show every extreme that they name: Exactly 8 tiles have corner_open = 0.
All inputs are finite; a program needn't handle non-finite values.
Results may differ from the reference program's by a relative error of at most 0.019.
The reference program's roundings to bfloat16 on the way count: a program that leaves them out, or rounds other values in their place, can miss the bound.
Values may be sent and summed in bfloat16 or wider, within the bound.
No kernel may reach another device: no remote copies, remote signals or barrier semaphores. Data moves between devices by JAX's collectives and lax.ppermute only.
A program may use at most 64 MiB of HBM per device.

```python
from functools import partial
import jax
import jax.numpy as jnp
from jax import lax

D = 1024
HEADS = 8
HD = 64
WIN = 8
GRID_COLS = 8
VERTICES = 8
TILE_SIDE = 16
TILES = 64
SAMPLES = 8
N_FSDP = 8


def draw_w_qkv(key, part):
    key = jax.random.fold_in(key, 11)
    base = jax.random.normal(key, (D, 3 * HEADS * HD), jnp.float32) * D ** (-0.5)
    return base.astype(jnp.bfloat16)


def draw_corner_open(key, part):
    key = jax.random.fold_in(key, 12)
    shuffled = jax.random.permutation(key, TILES)
    return (shuffled >= VERTICES).astype(jnp.int32)


def with_ends(array, key, low, high):
    dims = array.shape
    index_at = [jax.random.randint(jax.random.fold_in(key, axis), (), 0, dims[axis]) for axis in range(len(dims))]
    array = array.at[tuple(index_at)].set(low)
    longest = dims.index(max(dims))
    index_at[longest] = (index_at[longest] + 1) % dims[longest]
    return array.at[tuple(index_at)].set(high)


def block_levels(rng, shape, shards, low, largest):
    factor_of = 1.0
    for dim, shards_of in shards:
        heights = jax.random.uniform(jax.random.fold_in(jax.random.fold_in(rng, 6), dim), (shards_of,), jnp.float32, low / len(shards), largest / len(shards))
        factor_of = factor_of * jnp.repeat(jnp.exp(heights), shape[dim] // shards_of).reshape((-1,) + (1,) * (len(shape) - 1 - dim))
    return factor_of


def bell_draw(key, dims, scale, reach, pieces=(), kind=jnp.bfloat16):
    array = scale * jax.random.normal(key, dims, jnp.float32)
    if pieces:
        array = array * block_levels(key, dims, pieces, -0.22, 0.18)
    return jnp.clip(array, -reach, reach).astype(kind)


def setup_inputs(seed: int = 0) -> dict:
    arg_keys = jax.random.split(jax.random.key(seed), 8)
    return {
        "tokens": bell_draw(arg_keys[0], (SAMPLES, TILES, TILE_SIDE, TILE_SIDE, D), 1.0, 6.0, ((0, 8), (1, 64))),
        "w_qkv": draw_w_qkv(jax.random.fold_in(arg_keys[7], 71), 0),
        "w_out": bell_draw(arg_keys[2], (HEADS * HD, D), (HEADS * HD) ** -0.5, 0.25, ((0, 8),)),
        "rel_bias": bell_draw(arg_keys[3], (HEADS, 2 * WIN - 1, 2 * WIN - 1), 1.0, 4.0, (), jnp.float32),
        "seam_codes": with_ends(jax.random.randint(arg_keys[4], (TILES, 3), 0, 4), jax.random.fold_in(arg_keys[4], 1), 0, 3).astype(jnp.int32),
        "corner_open": draw_corner_open(jax.random.fold_in(arg_keys[7], 71), 0),
        "grad_out": bell_draw(arg_keys[6], (SAMPLES, TILES, TILE_SIDE, TILE_SIDE, D), 1.0, 6.0, ((0, 8), (1, 64))),
    }


EPSILON = 1e-05

def position_bias(rel_bias):
    span = 2 * WIN - 1
    places = jnp.arange(WIN * WIN, dtype=jnp.int32)
    row_of = places // WIN
    col_of = places % WIN
    offset = (row_of[:, None] - row_of[None, :] + WIN - 1) * span + (col_of[:, None] - col_of[None, :] + WIN - 1)
    onehot = (offset.reshape(-1)[:, None] == jnp.arange(span * span, dtype=jnp.int32)[None, :]).astype(jnp.float32)
    table = rel_bias.astype(jnp.float32).reshape(HEADS, span * span)
    picked = jnp.dot(onehot, table.T, precision=lax.Precision.HIGHEST, preferred_element_type=jnp.float32)
    return picked.T.reshape(HEADS, WIN * WIN, WIN * WIN)

def orient_strip(strip, seam_code, along, across):
    strip = jnp.where(seam_code % 2 == 1, jnp.flip(strip, along), strip)
    return jnp.where(seam_code // 2 == 1, jnp.flip(strip, across), strip)

def turn_corner(corner_cells, seam_code):
    result = corner_cells
    for turns in range(1, 4):
        result = jnp.where(seam_code == turns, jnp.rot90(corner_cells, turns, axes=(0, 1)), result)
    return result

def assemble(own_block, east_strip, south_strip, corner_cells, tile_codes):
    east_strip = orient_strip(east_strip, tile_codes[0], 0, 1)
    south_strip = orient_strip(south_strip, tile_codes[1], 1, 0)
    corner_cells = turn_corner(corner_cells, tile_codes[2])
    upper = jnp.concatenate([own_block, east_strip], 1)
    lower = jnp.concatenate([south_strip, corner_cells], 1)
    return jnp.concatenate([upper, lower], 0)

def disassemble(region, tile_codes, inner_len):
    own_block = region[:inner_len, :inner_len]
    east_strip = orient_strip(region[:inner_len, inner_len:], tile_codes[0], 0, 1)
    south_strip = orient_strip(region[inner_len:, :inner_len], tile_codes[1], 1, 0)
    corner_cells = turn_corner(region[inner_len:, inner_len:], (4 - tile_codes[2]) % 4)
    return (own_block, east_strip, south_strip, corner_cells)

def place_home(own_block, west_part, north_part, corner_part, row_axis):
    upper = jnp.concatenate([corner_part, north_part], row_axis + 1)
    lower = jnp.concatenate([west_part, own_block], row_axis + 1)
    return jnp.concatenate([upper, lower], row_axis)

def region_mask(side_len, inner_len, open_flag):
    rows = lax.broadcasted_iota(jnp.int32, (side_len, side_len), 0)
    columns = lax.broadcasted_iota(jnp.int32, (side_len, side_len), 1)
    return (open_flag == 1) | (rows < inner_len) | (columns < inner_len)

def split_windows(blocks_in, window):
    side_len = blocks_in.shape[0]
    number = side_len // window
    width = blocks_in.shape[-1]
    blocks_in = blocks_in.reshape(number, window, number, window, width)
    return blocks_in.transpose(0, 2, 1, 3, 4).reshape(number * number, window * window, width)

def merge_windows(blocks_in, side_len, window):
    number = side_len // window
    width = blocks_in.shape[-1]
    blocks_in = blocks_in.reshape(number, number, window, window, width).transpose(0, 2, 1, 3, 4)
    return blocks_in.reshape(side_len * side_len, width)

def normalize(tokens_flat):
    values = tokens_flat.astype(jnp.float32)
    center = values - lax.optimization_barrier(jnp.mean(values, -1, keepdims=True))
    variance = lax.optimization_barrier(jnp.mean(center * center, -1, keepdims=True))
    inverse = lax.rsqrt(variance + EPSILON)
    return (center * inverse, inverse)

def round_trip(values):
    return lax.optimization_barrier(values.astype(jnp.bfloat16)).astype(jnp.float32)

def region_pass(region_x, region_dy, valid_cells, w_qkv, w_out, bias_full):
    side_len = region_x.shape[0]
    cell_count = side_len * side_len
    flat_x = region_x.reshape(cell_count, -1)
    normed_f, inverse = normalize(flat_x)
    normed = normed_f.astype(jnp.bfloat16)
    qkv = jnp.dot(normed, w_qkv, preferred_element_type=jnp.float32).astype(jnp.bfloat16)
    window_qkv = split_windows(qkv.reshape(side_len, side_len, -1), WIN).reshape(-1, WIN * WIN, HEADS, 3, HD)
    window_valid = split_windows(valid_cells[:, :, None].astype(jnp.int32), WIN)[..., 0] == 1
    queries = window_qkv[:, :, :, 0].astype(jnp.float32)
    keys_part = window_qkv[:, :, :, 1].astype(jnp.float32)
    values_part = window_qkv[:, :, :, 2].astype(jnp.float32)
    scores = jnp.einsum('wqhd,wkhd->whqk', queries, keys_part) * HD ** (-0.5) + bias_full[None]
    scores = jnp.where(window_valid[:, None, None, :], scores, -1e+30)
    row_max = lax.optimization_barrier(jnp.max(scores, -1, keepdims=True))
    expo = jnp.exp(scores - row_max)
    attn_probs = expo / lax.optimization_barrier(jnp.sum(expo, -1, keepdims=True))
    attn_probs = attn_probs * window_valid[:, None, :, None].astype(jnp.float32)
    probs_f = round_trip(attn_probs)
    heads_w = jnp.einsum('whqk,wkhd->wqhd', probs_f, values_part).astype(jnp.bfloat16)
    heads_out = merge_windows(heads_w.reshape(-1, WIN * WIN, HEADS * HD), side_len, WIN)
    branch = jnp.dot(heads_out, w_out, preferred_element_type=jnp.float32).astype(jnp.bfloat16)
    flat_dy = region_dy.reshape(cell_count, -1)
    grad_heads = jnp.dot(flat_dy, w_out.T, preferred_element_type=jnp.float32).astype(jnp.bfloat16)
    out_term = jnp.dot(heads_out.T, flat_dy, preferred_element_type=jnp.float32)
    grad_w = split_windows(grad_heads.reshape(side_len, side_len, -1), WIN).reshape(-1, WIN * WIN, HEADS, HD).astype(jnp.float32)
    dprobs = jnp.einsum('wqhd,wkhd->whqk', grad_w, values_part)
    dvalues = jnp.einsum('whqk,wqhd->wkhd', probs_f, grad_w).astype(jnp.bfloat16)
    delta = lax.optimization_barrier(jnp.sum(dprobs * attn_probs, -1, keepdims=True))
    dscores = round_trip(attn_probs * (dprobs - delta) * HD ** (-0.5))
    dqueries = jnp.einsum('whqk,wkhd->wqhd', dscores, keys_part).astype(jnp.bfloat16)
    dkeys = jnp.einsum('whqk,wqhd->wkhd', dscores, queries).astype(jnp.bfloat16)
    dqkv_w = jnp.stack([dqueries, dkeys, dvalues], axis=3)
    dqkv = merge_windows(dqkv_w.reshape(-1, WIN * WIN, HEADS * 3 * HD), side_len, WIN)
    dnormed = jnp.dot(dqkv, w_qkv.T, preferred_element_type=jnp.float32)
    dnorm_in = inverse * (dnormed - lax.optimization_barrier(jnp.mean(dnormed, -1, keepdims=True)) - normed_f * lax.optimization_barrier(jnp.mean(dnormed * normed_f, -1, keepdims=True)))
    qkv_term = jnp.dot(normed.T, dqkv, preferred_element_type=jnp.float32)
    return (branch.reshape(side_len, side_len, -1), dnorm_in.reshape(side_len, side_len, -1), qkv_term, out_term)

def reference(tokens, w_qkv, w_out, rel_bias, seam_codes, corner_open, grad_out):
    side_len = TILE_SIDE
    half_win = WIN // 2
    inner_len = side_len - half_win
    bias_full = position_bias(rel_bias)

    def regions(source):
        east_src = jnp.roll(source, -1, axis=1)[:, :, half_win:, :half_win]
        south_src = jnp.roll(source, -GRID_COLS, axis=1)[:, :, :half_win, half_win:]
        corner_src = jnp.roll(source, -(GRID_COLS + 1), axis=1)[:, :, :half_win, :half_win]
        build = jax.vmap(jax.vmap(assemble, in_axes=(0, 0, 0, 0, None)), in_axes=(1, 1, 1, 1, 0), out_axes=1)
        return build(source[:, :, half_win:, half_win:], east_src, south_src, corner_src, seam_codes)

    def masks(open_flag):
        return region_mask(side_len, inner_len, open_flag)
    region_x = jnp.moveaxis(regions(tokens), 1, 0)
    region_dy = jnp.moveaxis(regions(grad_out), 1, 0)
    valid_all = jax.vmap(masks)(corner_open)

    def one_tile(carry, item):
        tile_x, tile_dy, tile_valid = item
        branch, dnorm_in, qkv_terms, out_terms = jax.vmap(region_pass, in_axes=(0, 0, None, None, None, None))(tile_x, tile_dy, tile_valid, w_qkv, w_out, bias_full)
        qkv_group = lax.optimization_barrier(jnp.sum(qkv_terms.reshape(N_FSDP, -1, D, 3 * HEADS * HD), axis=1))
        out_group = lax.optimization_barrier(jnp.sum(out_terms.reshape(N_FSDP, -1, HEADS * HD, D), axis=1))
        qkv_sum = carry[0] + lax.optimization_barrier(jnp.sum(round_trip(qkv_group), axis=0))
        out_sum = carry[1] + lax.optimization_barrier(jnp.sum(round_trip(out_group), axis=0))
        return ((qkv_sum, out_sum), (branch, dnorm_in))
    initial = (jnp.zeros((D, 3 * HEADS * HD), jnp.float32), jnp.zeros((HEADS * HD, D), jnp.float32))
    (grad_w_qkv, grad_w_out), (branch_all, dnorm_all) = lax.scan(one_tile, initial, (region_x, region_dy, valid_all))
    branch_all = jnp.moveaxis(branch_all, 0, 1)
    dnorm_all = jnp.moveaxis(dnorm_all, 0, 1)

    def send_home(region_vals):
        split = jax.vmap(jax.vmap(partial(disassemble, inner_len=inner_len), in_axes=(0, None)), in_axes=(1, 0), out_axes=1)
        own_block, east_strip, south_strip, corner_cells = split(region_vals, seam_codes)
        west_part = jnp.roll(east_strip, 1, axis=1)
        north_part = jnp.roll(south_strip, GRID_COLS, axis=1)
        corner_part = jnp.roll(corner_cells, GRID_COLS + 1, axis=1)
        return place_home(own_block, west_part, north_part, corner_part, 2)
    output = (tokens.astype(jnp.float32) + send_home(branch_all).astype(jnp.float32)).astype(jnp.bfloat16)
    grad_tokens = (grad_out.astype(jnp.float32) + send_home(dnorm_all)).astype(jnp.bfloat16)
    return (output, grad_tokens, grad_w_qkv, grad_w_out)
```

```python
import functools
import jax
import jax.numpy as jnp
from jax import lax
from jax.experimental import pallas as pl
from jax.experimental.pallas import tpu as pltpu
from jax.sharding import Mesh, PartitionSpec as P

HEADS = 8
HD = 64
WIN = 8
GRID_COLS = 8
SIDE = 16
HALF = WIN // 2
INNER = SIDE - HALF
CELLS = SIDE * SIDE
EAST = INNER * HALF
CORNER = HALF * HALF
EPSILON = 1e-05
NEG = -1e30
TRAILING = (((1,), (1,)), ((), ()))
LEADING = (((0,), (0,)), ((), ()))
VMEM_LIMIT = 56 * 1024 * 1024

f32 = jnp.float32
bf16 = jnp.bfloat16


def mm(a, b, dims=(((1,), (0,)), ((), ()))):
    return lax.dot_general(a, b, dims, preferred_element_type=f32)


def region_coords(shape, axis):
    place = lax.broadcasted_iota(jnp.int32, shape, axis)
    window, inside = place >> 6, place & 63
    row = (window >> 1) * WIN + (inside >> 3)
    column = (window & 1) * WIN + (inside & 7)
    return row, column


def source_of(codes, shape, axis):
    row, column = region_coords(shape, axis)
    flip_one, flip_two = codes[0] & 1, codes[0] >> 1
    er = jnp.where(flip_one == 1, INNER - 1 - row, row)
    ec = column - INNER
    ec = jnp.where(flip_two == 1, HALF - 1 - ec, ec)
    flip_one, flip_two = codes[1] & 1, codes[1] >> 1
    sc = jnp.where(flip_one == 1, INNER - 1 - column, column)
    sr = row - INNER
    sr = jnp.where(flip_two == 1, HALF - 1 - sr, sr)
    i, j = row - INNER, column - INNER
    turn = codes[2]
    last = HALF - 1
    cr = jnp.where(turn == 0, i, jnp.where(turn == 1, j, jnp.where(turn == 2, last - i, last - j)))
    cc = jnp.where(turn == 0, j, jnp.where(turn == 1, last - i, jnp.where(turn == 2, last - j, i)))
    own = (row + HALF) * SIDE + column + HALF
    east = CELLS + er * HALF + ec
    south = CELLS + EAST + sr * INNER + sc
    corner = CELLS + 2 * EAST + cr * HALF + cc
    low_row, low_column = row < INNER, column < INNER
    return jnp.where(
        low_row, jnp.where(low_column, own, east), jnp.where(low_column, south, corner)
    )


def onehot(condition):
    return jnp.where(condition, 1.0, 0.0).astype(bf16)


def gather_matrices(codes):
    source = source_of(codes, (CELLS, 1), 0)
    own = onehot(source == lax.broadcasted_iota(jnp.int32, (CELLS, CELLS), 1))
    halo = onehot(source - CELLS == lax.broadcasted_iota(jnp.int32, (CELLS, 128), 1))
    return own, halo


def scatter_matrices(codes):
    source = source_of(codes, (1, CELLS), 1)
    own = onehot(source == lax.broadcasted_iota(jnp.int32, (CELLS, CELLS), 0))
    halo = onehot(source - CELLS == lax.broadcasted_iota(jnp.int32, (128, CELLS), 0))
    return own, halo


def arrived_matrix():
    place = lax.broadcasted_iota(jnp.int32, (CELLS, 1), 0)
    row, column = place >> 4, place & 15
    west = (row - HALF) * HALF + column
    north = EAST + row * INNER + column - HALF
    corner = 2 * EAST + row * HALF + column
    low_row, low_column = row < HALF, column < HALF
    index = jnp.where(
        low_row,
        jnp.where(low_column, corner, north),
        jnp.where(low_column, west, -1),
    )
    return onehot(index == lax.broadcasted_iota(jnp.int32, (CELLS, 128), 1))


def prep_kernel(ints_ref, tok_ref, dy_ref, e_ref, s_ref, c_ref, normed_ref, normf_ref, inv_ref, rdy_ref):
    codes = [ints_ref[k] for k in range(3)]
    own, halo = gather_matrices(codes)
    pad = jnp.zeros((128 - 2 * EAST - CORNER, tok_ref.shape[1]), bf16)

    def region(main, which):
        edge = jnp.concatenate([e_ref[which], s_ref[which], c_ref[which], pad], axis=0)
        return mm(own, main) + mm(halo, edge)

    values = region(tok_ref[...], 0)
    center = values - jnp.mean(values, -1, keepdims=True)
    variance = jnp.mean(center * center, -1, keepdims=True)
    inverse = lax.rsqrt(variance + EPSILON)
    normed_f = center * inverse
    normf_ref[...] = normed_f
    normed_ref[...] = normed_f.astype(bf16)
    inv_ref[...] = jnp.broadcast_to(inverse, inv_ref.shape)
    rdy_ref[...] = region(dy_ref[...], 1).astype(bf16)


def attention(open_flag, qkv, grad_heads, bias_ref, heads_ref, dqkv_ref):
    rows = lax.broadcasted_iota(jnp.int32, (128, 128), 0)
    cols = lax.broadcasted_iota(jnp.int32, (128, 128), 1)
    same = (rows >> 6) == (cols >> 6)

    def closed(place):
        inside = place & 63
        return (place >= 64) & ((inside >> 3) >= HALF) & ((inside & 7) >= HALF)

    shut = open_flag == 0
    masks = [
        jnp.where(same, 0.0, NEG),
        jnp.where(same & jnp.logical_not(shut & closed(cols)), 0.0, NEG),
    ]
    place = lax.broadcasted_iota(jnp.int32, (128, 1), 0)
    keep = jnp.where(shut & closed(place), 0.0, 1.0)
    scale = HD ** (-0.5)
    for block in range(2):
        span = pl.ds(block * 128, 128)
        for pair in range(HEADS // 2):
            wide = qkv[span, pl.ds(pair * 384, 384)]
            grads = grad_heads[span, pl.ds(pair * 128, 128)]
            outs, parts = [], []
            for one in range(2):
                head = pair * 2 + one
                q = wide[:, one * 192 : one * 192 + 64]
                k = wide[:, one * 192 + 64 : one * 192 + 128]
                v = wide[:, one * 192 + 128 : one * 192 + 192]
                g = grads[:, one * 64 : one * 64 + 64]
                b64 = bias_ref[head]
                b = jnp.concatenate([b64, b64], axis=1)
                b = jnp.concatenate([b, b], axis=0)
                s = mm(q, k, TRAILING) * scale + b + masks[block]
                e = jnp.exp(s - jnp.max(s, -1, keepdims=True))
                probs = e / jnp.sum(e, -1, keepdims=True)
                if block == 1:
                    probs = probs * keep
                pb = probs.astype(bf16)
                outs.append(mm(pb, v).astype(bf16))
                dp = mm(g, v, TRAILING)
                dv = mm(pb, g, LEADING).astype(bf16)
                delta = jnp.sum(dp * probs, -1, keepdims=True)
                ds = (probs * (dp - delta) * scale).astype(bf16)
                dq = mm(ds, k).astype(bf16)
                dk = mm(ds, q, LEADING).astype(bf16)
                parts += [dq, dk, dv]
            heads_ref[span, pl.ds(pair * 128, 128)] = jnp.concatenate(outs, axis=1)
            dqkv_ref[span, pl.ds(pair * 384, 384)] = jnp.concatenate(parts, axis=1)


def main_kernel(ints_ref, normed_ref, rdy_ref, mine_ref, other_ref, bias_ref, dqkv_ref, heads_ref, qkv_ref, gh_ref):
    core = ints_ref[4]
    normed = normed_ref[...]
    for ref, owner in ((mine_ref, core), (other_ref, 1 - core)):
        for y in range(3):
            start = pl.multiple_of((y * 2 + owner) * 256, 256)
            qkv_ref[:, pl.ds(start, 256)] = mm(normed, ref[y]).astype(bf16)
    total = None
    for ref, owner in ((mine_ref, core), (other_ref, 1 - core)):
        for half in range(2):
            block = out_block(ref, half)
            start = pl.multiple_of(half * 512 + owner * 256, 256)
            term = mm(rdy_ref[:, pl.ds(start, 256)], block, TRAILING)
            total = term if total is None else total + term
    gh_ref[...] = total.astype(bf16)
    attention(ints_ref[3], qkv_ref, gh_ref, bias_ref, heads_ref, dqkv_ref)


def out_block(ref, half):
    return jnp.concatenate([ref[3, pl.ds(k * 128 + half * 64, 64)] for k in range(8)], axis=0)


def home_kernel(
    ints_ref, normf_ref, inv_ref, tok_ref, dy_ref, mine_ref, other_ref, dqkv_ref, heads_ref,
    out_ref, gtok_ref, east_ref, south_ref, corner_ref, branch_ref,
):
    core = ints_ref[4]
    own, halo = scatter_matrices([ints_ref[k] for k in range(3)])
    dnormed = None
    for ref, owner in ((mine_ref, core), (other_ref, 1 - core)):
        for half in range(2):
            start = pl.multiple_of(half * 512 + owner * 256, 256)
            branch_ref[:, pl.ds(start, 256)] = mm(heads_ref[...], out_block(ref, half)).astype(bf16)
        for y in range(3):
            start = pl.multiple_of((y * 2 + owner) * 256, 256)
            term = mm(dqkv_ref[:, pl.ds(start, 256)], ref[y], TRAILING)
            dnormed = term if dnormed is None else dnormed + term

    def edges(which, values):
        edge = mm(halo, values).astype(bf16)
        east_ref[which] = edge[:EAST]
        south_ref[which] = edge[EAST : 2 * EAST]
        corner_ref[which] = edge[2 * EAST : 2 * EAST + CORNER]

    branch = branch_ref[...]
    edges(0, branch)
    out_ref[...] = (tok_ref[...].astype(f32) + mm(own, branch)).astype(bf16)
    normed_f = normf_ref[...]
    dnorm = inv_ref[:, :1] * (
        dnormed
        - jnp.mean(dnormed, -1, keepdims=True)
        - normed_f * jnp.mean(dnormed * normed_f, -1, keepdims=True)
    )
    high = dnorm.astype(bf16)
    low = (dnorm - high.astype(f32)).astype(bf16)
    edges(1, high)
    gtok_ref[...] = (dy_ref[...].astype(f32) + (mm(own, high) + mm(own, low))).astype(bf16)


def finish_kernel(out_ref, gtok_ref, west_ref, north_ref, corner_ref, out2_ref, gtok2_ref):
    place = arrived_matrix()
    pad = jnp.zeros((128 - 2 * EAST - CORNER, out_ref.shape[1]), bf16)
    for which, (part, result) in enumerate(((out_ref, out2_ref), (gtok_ref, gtok2_ref))):
        edge = jnp.concatenate([west_ref[which], north_ref[which], corner_ref[which], pad], axis=0)
        result[...] = (part[...].astype(f32) + mm(place, edge)).astype(bf16)


def grads_kernel(ints_ref, normed_ref, rdy_ref, dqkv_ref, heads_ref, send_ref, keep_ref, tq_ref, to_ref):
    core = ints_ref[4]
    tq_ref[...] = mm(dqkv_ref[...], normed_ref[...], LEADING)
    heads = heads_ref[...]
    twice = []
    for head in range(HEADS):
        one = heads[:, head * HD : (head + 1) * HD]
        twice += [one, one]
    to_ref[...] = mm(rdy_ref[...], jnp.concatenate(twice, axis=1), LEADING)
    lower = lax.broadcasted_iota(jnp.int32, (8, 256), 1) & 127 < 64
    for out_ref, owner in ((send_ref, 1 - core), (keep_ref, core)):
        for y in range(4):
            for x in range(4):
                lanes = pl.ds(x * 256, 256)
                rows = [
                    tq_ref[pl.ds(pl.multiple_of(z * 192 + y * 48 + owner * 24, 8), 24), lanes]
                    for z in range(8)
                ]
                for z in range(8):
                    start = z * 128 + y * 32 + owner * 16
                    low = to_ref[pl.ds(pl.multiple_of(start, 8), 8), lanes]
                    high = to_ref[pl.ds(pl.multiple_of(start + 8, 8), 8), lanes]
                    rows.append(jnp.where(lower, low, high))
                out_ref[y, x] = jnp.concatenate(rows, axis=0).astype(bf16)


def pair_kernel(keep_ref, got_ref, out_ref):
    out_ref[...] = (keep_ref[...].astype(f32) + got_ref[...].astype(f32)).astype(bf16)


def plane_kernel(got_ref, out_ref):
    total = got_ref[0].astype(f32)
    for part in range(1, 16):
        total = total + got_ref[part].astype(f32)
    for z in range(8):
        rows = jnp.concatenate([total[z * 24 : z * 24 + 24], total[192 + z * 8 : 200 + z * 8]], axis=0)
        out_ref[z, 0] = rows[:, :128]
        out_ref[z, 1] = rows[:, 128:]


def last_kernel(got_ref, gq_ref, go_ref):
    total = got_ref[0]
    for part in range(1, 16):
        total = total + got_ref[part]
    square = jnp.concatenate([total, jnp.zeros((96, 128), f32)], axis=0).T
    gq_ref[...] = square[:, :24]
    go_ref[...] = jnp.concatenate([square[:64, 24:32], square[64:, 24:32]], axis=1)


def call(kernel, outs, *args, smem=0, scratch=(), flops=0, name=None):
    specs = [pl.BlockSpec(memory_space=pltpu.SMEM)] * smem + [pl.BlockSpec(memory_space=pltpu.VMEM)] * (
        len(args) - smem
    )
    shapes = [jax.ShapeDtypeStruct(s, d) for s, d in outs]
    size = sum(a.size * a.dtype.itemsize for a in (*args, *shapes))
    return pl.pallas_call(
        kernel,
        out_shape=shapes,
        in_specs=specs,
        out_specs=[pl.BlockSpec(memory_space=pltpu.VMEM)] * len(outs),
        scratch_shapes=list(scratch),
        compiler_params=pltpu.CompilerParams(vmem_limit_bytes=VMEM_LIMIT),
        cost_estimate=pl.CostEstimate(flops=flops, bytes_accessed=size, transcendentals=0),
        name=name,
    )(*args)


def position_bias(rel_bias):
    span = 2 * WIN - 1
    places = jnp.arange(WIN * WIN, dtype=jnp.int32)
    row_of = places // WIN
    col_of = places % WIN
    offset = (row_of[:, None] - row_of[None, :] + WIN - 1) * span + (
        col_of[:, None] - col_of[None, :] + WIN - 1
    )
    onehot_table = (
        offset.reshape(-1)[:, None] == jnp.arange(span * span, dtype=jnp.int32)[None, :]
    ).astype(f32)
    picked = jnp.dot(
        onehot_table,
        rel_bias.reshape(HEADS, span * span).T,
        precision=lax.Precision.HIGHEST,
        preferred_element_type=f32,
    )
    return picked.T.reshape(HEADS, WIN * WIN, WIN * WIN)


TILE_AXES = ("zl", "y", "c")


def shifted(block, distance):
    count = lax.axis_size(TILE_AXES)
    return lax.ppermute(block, TILE_AXES, [((i - distance) % count, i) for i in range(count)])


def per_device(tokens, w_qkv, w_out, rel_bias, seam_codes, corner_open, grad_out):
    width = tokens.shape[-1]
    both = jnp.stack([tokens[0, 0], grad_out[0, 0]])
    tok = tokens.reshape(CELLS, width)
    dy = grad_out.reshape(CELLS, width)
    core = lax.axis_index("c")
    ints = jnp.concatenate([seam_codes[0], corner_open, core[None]]).astype(jnp.int32)

    packed = jnp.concatenate(
        [w_qkv, jnp.concatenate([w_out[:, :512], w_out[:, 512:]], axis=0)], axis=1
    )
    block_at = (lax.axis_index("y") * 2 + core) * 256
    piece = lax.dynamic_slice(packed, (0, block_at), (128, 256))
    across = lax.ppermute(piece, "zh", [(0, 1), (1, 0)])
    first = lax.axis_index("zh") == 0
    piece = jnp.stack([jnp.where(first, piece, across), jnp.where(first, across, piece)])
    mine = lax.all_to_all(
        jnp.broadcast_to(piece[None], (16, 2, 128, 256)), ("y", "x"), 0, 0, tiled=True
    ).reshape(4, width, 256)
    other = lax.ppermute(mine, "c", [(0, 1), (1, 0)])

    east = shifted(both[:, HALF:, :HALF].reshape(2, EAST, width), -1)
    south = shifted(both[:, :HALF, HALF:].reshape(2, EAST, width), -GRID_COLS)
    corner = shifted(both[:, :HALF, :HALF].reshape(2, CORNER, width), -(GRID_COLS + 1))
    bias = position_bias(rel_bias)
    normed, normed_f, inverse, region_dy = call(
        prep_kernel,
        [((CELLS, width), bf16), ((CELLS, width), f32), ((CELLS, 128), f32), ((CELLS, width), bf16)],
        ints, tok, dy, east, south, corner,
        smem=1, flops=4 * 256 * 384 * 1024, name="prep",
    )
    dqkv, heads = call(
        main_kernel,
        [((CELLS, 1536), bf16), ((CELLS, 512), bf16)],
        ints, normed, region_dy, mine, other, bias,
        smem=1, scratch=[pltpu.VMEM((CELLS, 1536), bf16), pltpu.VMEM((CELLS, 512), bf16)],
        flops=2 * 256 * 1024 * 2048, name="attend",
    )
    send, keep = call(
        grads_kernel,
        [((4, 4, 256, 256), bf16), ((4, 4, 256, 256), bf16)],
        ints, normed, region_dy, dqkv, heads,
        smem=1, scratch=[pltpu.VMEM((1536, 1024), f32), pltpu.VMEM((1024, 1024), f32)],
        flops=2 * 256 * 1024 * 2560, name="weight_grads",
    )
    got = lax.ppermute(send, "c", [(0, 1), (1, 0)])
    out_part, gtok_part, east, south, corner = call(
        home_kernel,
        [
            ((CELLS, width), bf16), ((CELLS, width), bf16),
            ((2, EAST, width), bf16), ((2, EAST, width), bf16), ((2, CORNER, width), bf16),
        ],
        ints, normed_f, inverse, tok, dy, mine, other, dqkv, heads,
        smem=1, scratch=[pltpu.VMEM((CELLS, width), bf16)], flops=2 * 256 * 1024 * 2800, name="home",
    )
    west = shifted(east, 1)
    north = shifted(south, GRID_COLS)
    corner = shifted(corner, GRID_COLS + 1)
    (pair,) = call(pair_kernel, [((4, 4, 256, 256), bf16)], keep, got, name="pair_sum")
    plane = lax.all_to_all(pair.reshape(16, 256, 256), ("y", "x"), 0, 0, tiled=True)
    (plane,) = call(plane_kernel, [((8, 2, 32, 128), f32)], plane, name="plane_sum")
    column = lax.all_to_all(plane.reshape(16, 32, 128), ("zl", "zh"), 0, 0, tiled=True)
    grad_w_qkv, grad_w_out = call(
        last_kernel, [((128, 24), f32), ((64, 16), f32)], column, name="column_sum"
    )
    output, grad_tokens = call(
        finish_kernel, [((CELLS, width), bf16), ((CELLS, width), bf16)],
        out_part, gtok_part, west, north, corner, name="finish",
    )
    return (
        output.reshape(tokens.shape), grad_tokens.reshape(tokens.shape), grad_w_qkv, grad_w_out
    )


def solution(mesh):
    fine = Mesh(mesh.devices.reshape(8, 4, 2, 4, 2), ("zl", "y", "c", "x", "zh"))
    fsdp = ("x", "zh")
    acts = P(fsdp, TILE_AXES, None, None, None)
    return jax.shard_map(
        per_device,
        mesh=fine,
        in_specs=(
            acts, P(fsdp, None), P(fsdp, None), P(), P(TILE_AXES, None), P(TILE_AXES), acts,
        ),
        out_specs=(acts, acts, P(fsdp, TILE_AXES), P(fsdp, TILE_AXES)),
        check_vma=False,
    )
```

```python
import functools
import jax
import jax.numpy as jnp
from jax import lax
from jax.experimental import pallas as pl
from jax.experimental.pallas import tpu as pltpu
from jax.sharding import Mesh, PartitionSpec as P

HEADS = 8
HD = 64
WIN = 8
GRID_COLS = 8
SIDE = 16
HALF = WIN // 2
INNER = SIDE - HALF
CELLS = SIDE * SIDE
EAST = INNER * HALF
CORNER = HALF * HALF
EPSILON = 1e-05
NEG = -1e30
TRAILING = (((1,), (1,)), ((), ()))
LEADING = (((0,), (0,)), ((), ()))
VMEM_LIMIT = 56 * 1024 * 1024

f32 = jnp.float32
bf16 = jnp.bfloat16


def mm(a, b, dims=(((1,), (0,)), ((), ()))):
    return lax.dot_general(a, b, dims, preferred_element_type=f32)


def region_coords(shape, axis):
    place = lax.broadcasted_iota(jnp.int32, shape, axis)
    window, inside = place >> 6, place & 63
    row = (window >> 1) * WIN + (inside >> 3)
    column = (window & 1) * WIN + (inside & 7)
    return row, column


def source_of(codes, shape, axis):
    row, column = region_coords(shape, axis)
    flip_one, flip_two = codes[0] & 1, codes[0] >> 1
    er = jnp.where(flip_one == 1, INNER - 1 - row, row)
    ec = column - INNER
    ec = jnp.where(flip_two == 1, HALF - 1 - ec, ec)
    flip_one, flip_two = codes[1] & 1, codes[1] >> 1
    sc = jnp.where(flip_one == 1, INNER - 1 - column, column)
    sr = row - INNER
    sr = jnp.where(flip_two == 1, HALF - 1 - sr, sr)
    i, j = row - INNER, column - INNER
    turn = codes[2]
    last = HALF - 1
    cr = jnp.where(turn == 0, i, jnp.where(turn == 1, j, jnp.where(turn == 2, last - i, last - j)))
    cc = jnp.where(turn == 0, j, jnp.where(turn == 1, last - i, jnp.where(turn == 2, last - j, i)))
    own = (row + HALF) * SIDE + column + HALF
    east = CELLS + er * HALF + ec
    south = CELLS + EAST + sr * INNER + sc
    corner = CELLS + 2 * EAST + cr * HALF + cc
    low_row, low_column = row < INNER, column < INNER
    return jnp.where(
        low_row, jnp.where(low_column, own, east), jnp.where(low_column, south, corner)
    )


def onehot(condition):
    return jnp.where(condition, 1.0, 0.0).astype(bf16)


def gather_matrices(codes):
    source = source_of(codes, (CELLS, 1), 0)
    own = onehot(source == lax.broadcasted_iota(jnp.int32, (CELLS, CELLS), 1))
    halo = onehot(source - CELLS == lax.broadcasted_iota(jnp.int32, (CELLS, 128), 1))
    return own, halo


def scatter_matrices(codes):
    source = source_of(codes, (1, CELLS), 1)
    own = onehot(source == lax.broadcasted_iota(jnp.int32, (CELLS, CELLS), 0))
    halo = onehot(source - CELLS == lax.broadcasted_iota(jnp.int32, (128, CELLS), 0))
    return own, halo


def arrived_matrix():
    place = lax.broadcasted_iota(jnp.int32, (CELLS, 1), 0)
    row, column = place >> 4, place & 15
    west = (row - HALF) * HALF + column
    north = EAST + row * INNER + column - HALF
    corner = 2 * EAST + row * HALF + column
    low_row, low_column = row < HALF, column < HALF
    index = jnp.where(
        low_row,
        jnp.where(low_column, corner, north),
        jnp.where(low_column, west, -1),
    )
    return onehot(index == lax.broadcasted_iota(jnp.int32, (CELLS, 128), 1))


def prep_kernel(ints_ref, tok_ref, dy_ref, e_ref, s_ref, c_ref, sides_ref, normf_ref, inv_ref):
    codes = [ints_ref[k] for k in range(3)]
    own, halo = gather_matrices(codes)
    pad = jnp.zeros((128 - 2 * EAST - CORNER, tok_ref.shape[1]), bf16)

    def region(main, which):
        edge = jnp.concatenate([e_ref[which], s_ref[which], c_ref[which], pad], axis=0)
        return mm(own, main) + mm(halo, edge)

    values = region(tok_ref[...], 0)
    center = values - jnp.mean(values, -1, keepdims=True)
    variance = jnp.mean(center * center, -1, keepdims=True)
    inverse = lax.rsqrt(variance + EPSILON)
    normed_f = center * inverse
    normf_ref[...] = normed_f
    sides_ref[0] = normed_f.astype(bf16)
    inv_ref[...] = jnp.broadcast_to(inverse, inv_ref.shape)
    sides_ref[1] = region(dy_ref[...], 1).astype(bf16)


def attention(open_flag, qkv, grad_heads, bias_ref, back_ref):
    keys = lax.broadcasted_iota(jnp.int32, (128, 128), 0)
    queries = lax.broadcasted_iota(jnp.int32, (128, 128), 1)
    lower = lax.broadcasted_iota(jnp.int32, (64, 128), 1) < 64

    def closed(place):
        inside = place & 63
        return (place >= 64) & ((inside >> 3) >= HALF) & ((inside & 7) >= HALF)

    shut = open_flag == 0
    no_key = jnp.where(shut & closed(keys), NEG, 0.0)
    query = lax.broadcasted_iota(jnp.int32, (1, 128), 1)
    keep = jnp.where(shut & closed(query), 0.0, 1.0)
    scale = jnp.asarray(HD ** (-0.5), bf16)
    for pair in range(HEADS // 2):
        tables = []
        for one in range(2):
            table = bias_ref[pair * 2 + one]
            tables.append(jnp.concatenate([jnp.where(lower, table, NEG), jnp.where(lower, NEG, table)], axis=0))
        units = [(block, one) for block in range(2) for one in range(2)]
        q, k, v, g = [], [], [], []
        for block, one in units:
            span = pl.ds(block * 128, 128)
            wide = qkv[span, pl.ds(pair * 384, 384)]
            part = [wide[:, one * 192 + p * 64 : one * 192 + p * 64 + 64] for p in range(3)]
            q.append(part[0] * scale)
            k.append(part[1])
            v.append(part[2])
            g.append(grad_heads[span, pl.ds(pair * 128, 128)][:, one * 64 : one * 64 + 64])
        n = range(4)
        s = [mm(k[u], q[u], TRAILING) + tables[units[u][1]] for u in n]
        s = [s[u] + no_key if units[u][0] == 1 else s[u] for u in n]
        dp = [mm(v[u], g[u], TRAILING) for u in n]
        e = [jnp.exp(s[u] - jnp.max(s[u], 0, keepdims=True)) for u in n]
        r = [1.0 / jnp.sum(e[u], 0, keepdims=True) for u in n]
        r = [r[u] * keep if units[u][0] == 1 else r[u] for u in n]
        probs = [e[u] * r[u] for u in n]
        pb = [probs[u].astype(bf16) for u in n]
        ds = [
            (probs[u] * (dp[u] - jnp.sum(dp[u] * probs[u], 0, keepdims=True))).astype(bf16) for u in n
        ]
        out = [mm(pb[u], v[u], LEADING).astype(bf16) for u in n]
        dv = [mm(pb[u], g[u]).astype(bf16) for u in n]
        dq = [mm(ds[u], k[u] * scale, LEADING).astype(bf16) for u in n]
        dk = [mm(ds[u], q[u]).astype(bf16) for u in n]
        for block in range(2):
            span, u = pl.ds(block * 128, 128), block * 2
            back_ref[span, pl.ds(1536 + pair * 128, 128)] = jnp.concatenate([out[u], out[u + 1]], axis=1)
            back_ref[span, pl.ds(pair * 384, 384)] = jnp.concatenate(
                [dq[u], dk[u], dv[u], dq[u + 1], dk[u + 1], dv[u + 1]], axis=1
            )


def main_kernel(ints_ref, sides_ref, mine_ref, other_ref, bias_ref, back_ref, qkv_ref, gh_ref):
    core = ints_ref[4]
    normed = sides_ref[0]
    for ref, owner in ((mine_ref, core), (other_ref, 1 - core)):
        for y in range(3):
            start = pl.multiple_of((y * 2 + owner) * 256, 256)
            qkv_ref[:, pl.ds(start, 256)] = mm(normed, ref[y]).astype(bf16)
    total = None
    for ref, owner in ((mine_ref, core), (other_ref, 1 - core)):
        for half in range(2):
            start = pl.multiple_of(half * 512 + owner * 256, 256)
            term = mm(sides_ref[1, :, pl.ds(start, 256)], out_block(ref, half), TRAILING)
            total = term if total is None else total + term
    gh_ref[...] = total.astype(bf16)
    attention(ints_ref[3], qkv_ref, gh_ref, bias_ref, back_ref)


def out_block(ref, half):
    return jnp.concatenate([ref[3, pl.ds(k * 128 + half * 64, 64)] for k in range(8)], axis=0)


def home_kernel(
    ints_ref, normf_ref, inv_ref, tok_ref, dy_ref, mine_ref, other_ref, back_ref,
    out_ref, gtok_ref, east_ref, south_ref, corner_ref, branch_ref,
):
    core = ints_ref[4]
    own, halo = scatter_matrices([ints_ref[k] for k in range(3)])
    heads = back_ref[:, 1536:]
    dnormed = None
    for ref, owner in ((mine_ref, core), (other_ref, 1 - core)):
        for half in range(2):
            start = pl.multiple_of(half * 512 + owner * 256, 256)
            branch_ref[:, pl.ds(start, 256)] = mm(heads, out_block(ref, half)).astype(bf16)
        for y in range(3):
            start = pl.multiple_of((y * 2 + owner) * 256, 256)
            term = mm(back_ref[:, pl.ds(start, 256)], ref[y], TRAILING)
            dnormed = term if dnormed is None else dnormed + term

    def edges(which, values):
        edge = mm(halo, values).astype(bf16)
        east_ref[which] = edge[:EAST]
        south_ref[which] = edge[EAST : 2 * EAST]
        corner_ref[which] = edge[2 * EAST : 2 * EAST + CORNER]

    branch = branch_ref[...]
    edges(0, branch)
    out_ref[...] = (tok_ref[...].astype(f32) + mm(own, branch)).astype(bf16)
    normed_f = normf_ref[...]
    dnorm = inv_ref[:, :1] * (
        dnormed
        - jnp.mean(dnormed, -1, keepdims=True)
        - normed_f * jnp.mean(dnormed * normed_f, -1, keepdims=True)
    )
    high = dnorm.astype(bf16)
    low = (dnorm - high.astype(f32)).astype(bf16)
    edges(1, high)
    gtok_ref[...] = (dy_ref[...].astype(f32) + (mm(own, high) + mm(own, low))).astype(bf16)


def finish_kernel(out_ref, gtok_ref, west_ref, north_ref, corner_ref, out2_ref, gtok2_ref):
    place = arrived_matrix()
    pad = jnp.zeros((128 - 2 * EAST - CORNER, out_ref.shape[1]), bf16)
    for which, (part, result) in enumerate(((out_ref, out2_ref), (gtok_ref, gtok2_ref))):
        edge = jnp.concatenate([west_ref[which], north_ref[which], corner_ref[which], pad], axis=0)
        result[...] = (part[...].astype(f32) + mm(place, edge)).astype(bf16)


def grads_kernel(ints_ref, sides_ref, back_ref, peer_sides_ref, peer_back_ref, out_ref, tq_ref, to_ref):
    core = ints_ref[4]

    def two(ref, peer_ref, index):
        return jnp.concatenate([ref[index], peer_ref[index]], axis=0)

    back = (slice(None), slice(0, 1536))
    tq_ref[...] = mm(two(back_ref, peer_back_ref, back), two(sides_ref, peer_sides_ref, 0), LEADING)
    heads = two(back_ref, peer_back_ref, (slice(None), slice(1536, 2048)))
    twice = []
    for head in range(HEADS):
        one = heads[:, head * HD : (head + 1) * HD]
        twice += [one, one]
    to_ref[...] = mm(two(sides_ref, peer_sides_ref, 1), jnp.concatenate(twice, axis=1), LEADING)
    lower = lax.broadcasted_iota(jnp.int32, (8, 256), 1) & 127 < 64
    for y in range(4):
        for x in range(4):
            lanes = pl.ds(x * 256, 256)
            rows = [
                tq_ref[pl.ds(pl.multiple_of(z * 192 + y * 48 + core * 24, 8), 24), lanes]
                for z in range(8)
            ]
            for z in range(8):
                start = z * 128 + y * 32 + core * 16
                low = to_ref[pl.ds(pl.multiple_of(start, 8), 8), lanes]
                high = to_ref[pl.ds(pl.multiple_of(start + 8, 8), 8), lanes]
                rows.append(jnp.where(lower, low, high))
            out_ref[y, x] = jnp.concatenate(rows, axis=0).astype(bf16)


def plane_kernel(got_ref, out_ref, total_ref):
    step = pl.program_id(0)
    total = got_ref[0].astype(f32)
    for part in range(1, 16):
        total = total + got_ref[part].astype(f32)
    total_ref[pl.ds(pl.multiple_of(step * 64, 64), 64)] = total

    @pl.when(step == 3)
    def _():
        for z in range(8):
            for half in range(2):
                lanes = pl.ds(half * 128, 128)
                out_ref[z, half, :24] = total_ref[pl.ds(z * 24, 24), lanes]
                out_ref[z, half, 24:] = total_ref[pl.ds(192 + z * 8, 8), lanes]


def last_kernel(got_ref, gq_ref, go_ref):
    total = got_ref[0]
    for part in range(1, 16):
        total = total + got_ref[part]
    gq_ref[...] = total[:24]
    go_ref[...] = jnp.concatenate([total[24:, :64], total[24:, 64:]], axis=0)


def call(kernel, outs, *args, smem=0, scratch=(), flops=0, name=None):
    specs = [pl.BlockSpec(memory_space=pltpu.SMEM)] * smem + [pl.BlockSpec(memory_space=pltpu.VMEM)] * (
        len(args) - smem
    )
    shapes = [jax.ShapeDtypeStruct(s, d) for s, d in outs]
    size = sum(a.size * a.dtype.itemsize for a in (*args, *shapes))
    return pl.pallas_call(
        kernel,
        out_shape=shapes,
        in_specs=specs,
        out_specs=[pl.BlockSpec(memory_space=pltpu.VMEM)] * len(outs),
        scratch_shapes=list(scratch),
        compiler_params=pltpu.CompilerParams(vmem_limit_bytes=VMEM_LIMIT),
        cost_estimate=pl.CostEstimate(flops=flops, bytes_accessed=size, transcendentals=0),
        name=name,
    )(*args)


def position_bias(rel_bias):
    span = 2 * WIN - 1
    places = jnp.arange(WIN * WIN, dtype=jnp.int32)
    row_of = places // WIN
    col_of = places % WIN
    offset = (row_of[None, :] - row_of[:, None] + WIN - 1) * span + (
        col_of[None, :] - col_of[:, None] + WIN - 1
    )
    onehot_table = (
        offset.reshape(-1)[:, None] == jnp.arange(span * span, dtype=jnp.int32)[None, :]
    ).astype(f32)
    picked = jnp.dot(
        onehot_table,
        rel_bias.reshape(HEADS, span * span).T,
        precision=lax.Precision.HIGHEST,
        preferred_element_type=f32,
    )
    table = picked.T.reshape(HEADS, WIN * WIN, WIN * WIN)
    return jnp.concatenate([table, table], axis=2)


TILE_AXES = ("zl", "y", "c")


def shifted(block, distance):
    count = lax.axis_size(TILE_AXES)
    return lax.ppermute(block, TILE_AXES, [((i - distance) % count, i) for i in range(count)])


def per_device(tokens, w_qkv, w_out, rel_bias, seam_codes, corner_open, grad_out):
    width = tokens.shape[-1]
    both = jnp.stack([tokens[0, 0], grad_out[0, 0]])
    tok = tokens.reshape(CELLS, width)
    dy = grad_out.reshape(CELLS, width)
    core = lax.axis_index("c")
    ints = jnp.concatenate([seam_codes[0], corner_open, core[None]]).astype(jnp.int32)

    packed = jnp.concatenate(
        [w_qkv, jnp.concatenate([w_out[:, :512], w_out[:, 512:]], axis=0)], axis=1
    )
    block_at = (lax.axis_index("y") * 2 + core) * 256
    piece = lax.dynamic_slice(packed, (0, block_at), (128, 256))
    across = lax.ppermute(piece, "zh", [(0, 1), (1, 0)])
    first = lax.axis_index("zh") == 0
    piece = jnp.stack([jnp.where(first, piece, across), jnp.where(first, across, piece)])
    many = jnp.broadcast_to(piece[None], (16, 2, 128, 256))
    bias = position_bias(rel_bias)
    many, both, bias, ints = lax.optimization_barrier((many, both, bias, ints))
    mine = lax.all_to_all(many, ("y", "x"), 0, 0, tiled=True).reshape(4, width, 256)

    def swapped(block):
        return lax.ppermute(block, "c", [(0, 1), (1, 0)])

    east = shifted(both[:, HALF:, :HALF].reshape(2, EAST, width), -1)
    south = shifted(both[:, :HALF, HALF:].reshape(2, EAST, width), -GRID_COLS)
    corner = shifted(both[:, :HALF, :HALF].reshape(2, CORNER, width), -(GRID_COLS + 1))
    sides, normed_f, inverse = call(
        prep_kernel,
        [((2, CELLS, width), bf16), ((CELLS, width), f32), ((CELLS, 128), f32)],
        ints, tok, dy, east, south, corner,
        smem=1, flops=4 * 256 * 384 * 1024, name="prep",
    )
    mine, sides = lax.optimization_barrier((mine, sides))
    other = swapped(mine)
    peer_sides = swapped(sides)
    (back,) = call(
        main_kernel,
        [((CELLS, 2048), bf16)],
        ints, sides, mine, other, bias,
        smem=1, scratch=[pltpu.VMEM((CELLS, 1536), bf16), pltpu.VMEM((CELLS, 512), bf16)],
        flops=2 * 256 * 1024 * 2048, name="attend",
    )
    peer_back = swapped(back)
    (pair,) = call(
        grads_kernel,
        [((4, 4, 256, 256), bf16)],
        ints, sides, back, peer_sides, peer_back,
        smem=1, scratch=[pltpu.VMEM((1536, 1024), f32), pltpu.VMEM((1024, 1024), f32)],
        flops=2 * 512 * 1024 * 2560, name="weight_grads",
    )
    out_part, gtok_part, east, south, corner = call(
        home_kernel,
        [
            ((CELLS, width), bf16), ((CELLS, width), bf16),
            ((2, EAST, width), bf16), ((2, EAST, width), bf16), ((2, CORNER, width), bf16),
        ],
        ints, normed_f, inverse, tok, dy, mine, other, back,
        smem=1, scratch=[pltpu.VMEM((CELLS, width), bf16)], flops=2 * 256 * 1024 * 2800, name="home",
    )
    west = shifted(east, 1)
    north = shifted(south, GRID_COLS)
    corner = shifted(corner, GRID_COLS + 1)
    plane = lax.all_to_all(pair.reshape(16, 256, 256), ("y", "x"), 0, 0, tiled=True)
    plane, west, north, corner = lax.optimization_barrier((plane, west, north, corner))
    plane = pl.pallas_call(
        plane_kernel,
        grid=(4,),
        out_shape=jax.ShapeDtypeStruct((8, 2, 32, 128), f32),
        in_specs=[pl.BlockSpec((16, 64, 256), lambda i: (0, i, 0))],
        out_specs=pl.BlockSpec((8, 2, 32, 128), lambda i: (0, 0, 0, 0)),
        scratch_shapes=[pltpu.VMEM((256, 256), f32)],
        compiler_params=pltpu.CompilerParams(vmem_limit_bytes=VMEM_LIMIT),
        cost_estimate=pl.CostEstimate(flops=0, bytes_accessed=2**21, transcendentals=0),
        name="plane_sum",
    )(plane)
    column = lax.all_to_all(plane.reshape(16, 32, 128), ("zl", "zh"), 0, 0, tiled=True)
    grad_w_qkv, grad_w_out = call(
        last_kernel, [((24, 128), f32), ((16, 64), f32)], column, name="column_sum"
    )
    output, grad_tokens = call(
        finish_kernel, [((CELLS, width), bf16), ((CELLS, width), bf16)],
        out_part, gtok_part, west, north, corner, name="finish",
    )
    return (
        output.reshape(tokens.shape), grad_tokens.reshape(tokens.shape), grad_w_qkv.T, grad_w_out.T
    )


def solution(mesh):
    fine = Mesh(mesh.devices.reshape(8, 4, 2, 4, 2), ("zl", "y", "c", "x", "zh"))
    fsdp = ("x", "zh")
    acts = P(fsdp, TILE_AXES, None, None, None)
    return jax.shard_map(
        per_device,
        mesh=fine,
        in_specs=(
            acts, P(fsdp, None), P(fsdp, None), P(), P(TILE_AXES, None), P(TILE_AXES), acts,
        ),
        out_specs=(acts, acts, P(fsdp, TILE_AXES), P(fsdp, TILE_AXES)),
        check_vma=False,
    )
```

```python
import functools
import jax
import jax.numpy as jnp
from jax import lax
from jax.experimental import pallas as pl
from jax.experimental.pallas import tpu as pltpu
from jax.sharding import Mesh, PartitionSpec as P

HEADS = 8
HD = 64
WIN = 8
GRID_COLS = 8
SIDE = 16
HALF = WIN // 2
INNER = SIDE - HALF
CELLS = SIDE * SIDE
FLAG_ROWS = 16
EAST = INNER * HALF
CORNER = HALF * HALF
EPSILON = 1e-05
NEG = -1e30
TRAILING = (((1,), (1,)), ((), ()))
LEADING = (((0,), (0,)), ((), ()))
VMEM_LIMIT = 56 * 1024 * 1024

f32 = jnp.float32
bf16 = jnp.bfloat16


def mm(a, b, dims=(((1,), (0,)), ((), ()))):
    return lax.dot_general(a, b, dims, preferred_element_type=f32)


def region_coords(shape, axis):
    place = lax.broadcasted_iota(jnp.int32, shape, axis)
    window, inside = place >> 6, place & 63
    row = (window >> 1) * WIN + (inside >> 3)
    column = (window & 1) * WIN + (inside & 7)
    return row, column


def source_of(codes, shape, axis):
    row, column = region_coords(shape, axis)
    flip_one, flip_two = codes[0] & 1, codes[0] >> 1
    er = jnp.where(flip_one == 1, INNER - 1 - row, row)
    ec = column - INNER
    ec = jnp.where(flip_two == 1, HALF - 1 - ec, ec)
    flip_one, flip_two = codes[1] & 1, codes[1] >> 1
    sc = jnp.where(flip_one == 1, INNER - 1 - column, column)
    sr = row - INNER
    sr = jnp.where(flip_two == 1, HALF - 1 - sr, sr)
    i, j = row - INNER, column - INNER
    turn = codes[2]
    last = HALF - 1
    cr = jnp.where(turn == 0, i, jnp.where(turn == 1, j, jnp.where(turn == 2, last - i, last - j)))
    cc = jnp.where(turn == 0, j, jnp.where(turn == 1, last - i, jnp.where(turn == 2, last - j, i)))
    own = (row + HALF) * SIDE + column + HALF
    east = CELLS + er * HALF + ec
    south = CELLS + EAST + sr * INNER + sc
    corner = CELLS + 2 * EAST + cr * HALF + cc
    low_row, low_column = row < INNER, column < INNER
    return jnp.where(
        low_row, jnp.where(low_column, own, east), jnp.where(low_column, south, corner)
    )


def onehot(condition):
    return jnp.where(condition, 1.0, 0.0).astype(bf16)


def gather_matrices(codes):
    source = source_of(codes, (CELLS, 1), 0)
    own = onehot(source == lax.broadcasted_iota(jnp.int32, (CELLS, CELLS), 1))
    halo = onehot(source - CELLS == lax.broadcasted_iota(jnp.int32, (CELLS, 128), 1))
    return own, halo


def scatter_matrices(codes):
    source = source_of(codes, (1, CELLS), 1)
    own = onehot(source == lax.broadcasted_iota(jnp.int32, (CELLS, CELLS), 0))
    halo = onehot(source - CELLS == lax.broadcasted_iota(jnp.int32, (128, CELLS), 0))
    return own, halo


def arrived_matrix():
    place = lax.broadcasted_iota(jnp.int32, (CELLS, 1), 0)
    row, column = place >> 4, place & 15
    west = (row - HALF) * HALF + column
    north = EAST + row * INNER + column - HALF
    corner = 2 * EAST + row * HALF + column
    low_row, low_column = row < HALF, column < HALF
    index = jnp.where(
        low_row,
        jnp.where(low_column, corner, north),
        jnp.where(low_column, west, -1),
    )
    return onehot(index == lax.broadcasted_iota(jnp.int32, (CELLS, 128), 1))


def prep_kernel(ints_ref, tok_ref, dy_ref, e_ref, s_ref, c_ref, sides_ref, normf_ref, inv_ref):
    codes = [ints_ref[k] for k in range(3)]
    own, halo = gather_matrices(codes)
    pad = jnp.zeros((128 - 2 * EAST - CORNER, tok_ref.shape[1]), bf16)

    def region(main, which):
        edge = jnp.concatenate([e_ref[which], s_ref[which], c_ref[which], pad], axis=0)
        return mm(own, main) + mm(halo, edge)

    values = region(tok_ref[...], 0)
    center = values - jnp.mean(values, -1, keepdims=True)
    variance = jnp.mean(center * center, -1, keepdims=True)
    inverse = lax.rsqrt(variance + EPSILON)
    normed_f = center * inverse
    normf_ref[...] = normed_f
    sides_ref[0, :CELLS] = normed_f.astype(bf16)
    flag = jnp.where(ints_ref[3] == 0, 0.0, 1.0)
    sides_ref[0, CELLS:] = jnp.full((FLAG_ROWS, tok_ref.shape[1]), flag, f32).astype(bf16)
    sides_ref[1, CELLS:] = jnp.zeros((FLAG_ROWS, tok_ref.shape[1]), bf16)
    inv_ref[...] = jnp.broadcast_to(inverse, inv_ref.shape)
    sides_ref[1, :CELLS] = region(dy_ref[...], 1).astype(bf16)


def piece_kernel(spot_ref, wq_ref, wo_ref, out_ref):
    core, y = spot_ref[0], spot_ref[2]
    wq, wo = wq_ref[...], wo_ref[...]
    head = y * 2 + core
    part = wq[:, :192]
    for k in range(1, HEADS):
        part = jnp.where(head == k, wq[:, k * 192 : (k + 1) * 192], part)
    quarter = wo[:, :256]
    for k in range(1, 4):
        quarter = jnp.where(y == k, wo[:, k * 256 : (k + 1) * 256], quarter)
    group = [quarter[:, k * 64 : (k + 1) * 64] for k in range(4)]
    low = jnp.concatenate([group[0], group[2]], axis=1)
    high = jnp.concatenate([group[1], group[3]], axis=1)
    out_ref[...] = jnp.concatenate(
        [part, jnp.zeros((128, 64), bf16), jnp.concatenate([low, high], axis=0)], axis=1
    )


def slots_kernel(spot_ref, here_ref, there_ref, out_ref):
    core, zh = spot_ref[0], spot_ref[1]
    here, there = here_ref[...], there_ref[...]
    first = jnp.where(zh == 0, here, there)
    second = jnp.where(zh == 0, there, here)
    out = jnp.where(core == zh, here, there)[:, 256:]
    slot = jnp.concatenate(
        [
            jnp.concatenate([first[:, :192], out[:, :64]], axis=1),
            jnp.concatenate([second[:, :192], out[:, 64:]], axis=1),
        ],
        axis=0,
    )
    for k in range(16):
        out_ref[k] = slot


def attend_kernel(
    ints_ref, sides_ref, peer_ref, got_ref, bias_ref, back_ref, wo_ref, send_ref, qkv_ref, gh_ref
):
    core = ints_ref[4]
    both = [jnp.concatenate([sides_ref[k, :CELLS], peer_ref[k, :CELLS]], axis=0) for k in range(2)]
    for s in range(4):
        qkv_ref[:, pl.ds(s * 256, 256)] = mm(both[0], got_ref[s]).astype(bf16)
        for y in range(4):
            row = [got_ref[y, pl.ds(s * 256 + q * 64, 64), pl.ds(128, 128)][:, 64:] for q in range(4)]
            wo_ref[pl.ds(s * 64, 64), pl.ds(y * 256, 256)] = jnp.concatenate(row, axis=1)
    gh_ref[...] = mm(both[1], wo_ref[...], TRAILING).astype(bf16)
    keys = lax.broadcasted_iota(jnp.int32, (128, 128), 0)
    lower = lax.broadcasted_iota(jnp.int32, (64, 128), 1) < 64
    query = lax.broadcasted_iota(jnp.int32, (1, 128), 1)

    def closed(place):
        inside = place & 63
        return (place >= 64) & ((inside >> 3) >= HALF) & ((inside & 7) >= HALF)

    no_key, keep = [], []
    for ref in (sides_ref, peer_ref):
        flag = ref[0, CELLS:, :128].astype(f32)[:1]
        no_key.append(jnp.where(closed(keys) & (flag == 0.0), NEG, 0.0))
        keep.append(jnp.where(closed(query) & (flag == 0.0), 0.0, 1.0))
    scale = jnp.asarray(HD ** (-0.5), bf16)
    n = range(4)
    for head in range(4):
        table = bias_ref[head * 2 + core]
        table = jnp.concatenate([jnp.where(lower, table, NEG), jnp.where(lower, NEG, table)], axis=0)
        q, k, v, g = [], [], [], []
        for block in n:
            wide = qkv_ref[pl.ds(block * 128, 128), pl.ds(head * 256, 256)]
            q.append(wide[:, :64] * scale)
            k.append(wide[:, 64:128])
            v.append(wide[:, 128:192])
            pair = gh_ref[pl.ds(block * 128, 128), pl.ds(head // 2 * 128, 128)]
            g.append(pair[:, head % 2 * 64 : head % 2 * 64 + 64])
        score = [mm(k[u], q[u], TRAILING) + table for u in n]
        score = [score[u] + no_key[u // 2] if u % 2 == 1 else score[u] for u in n]
        dp = [mm(v[u], g[u], TRAILING) for u in n]
        e = [jnp.exp(score[u] - jnp.max(score[u], 0, keepdims=True)) for u in n]
        r = [1.0 / jnp.sum(e[u], 0, keepdims=True) for u in n]
        r = [r[u] * keep[u // 2] if u % 2 == 1 else r[u] for u in n]
        probs = [e[u] * r[u] for u in n]
        pb = [probs[u].astype(bf16) for u in n]
        ds = [
            (probs[u] * (dp[u] - jnp.sum(dp[u] * probs[u], 0, keepdims=True))).astype(bf16) for u in n
        ]
        out = [mm(pb[u], v[u], LEADING).astype(bf16) for u in n]
        dv = [mm(pb[u], g[u]).astype(bf16) for u in n]
        dq = [mm(ds[u], k[u] * scale, LEADING).astype(bf16) for u in n]
        dk = [mm(ds[u], q[u]).astype(bf16) for u in n]
        for u in n:
            back_ref[pl.ds(u * 128, 128), pl.ds(head * 256, 256)] = jnp.concatenate(
                [dq[u], dk[u], dv[u], out[u]], axis=1
            )
    branch, dnormed = head_parts(got_ref, wo_ref, back_ref[pl.ds(CELLS, CELLS)])
    send_ref[0] = branch.astype(bf16)
    send_ref[1] = dnormed.astype(bf16)


def grads_kernel(sides_ref, peer_ref, back_ref, out_ref, tq_ref, to_ref):
    both = [jnp.concatenate([sides_ref[k, :CELLS], peer_ref[k, :CELLS]], axis=0) for k in range(2)]
    back = back_ref[...]
    tq_ref[...] = mm(back, both[0], LEADING)
    twice = []
    for head in range(4):
        one = back[:, head * 256 + 192 : head * 256 + 256]
        twice += [one, one]
    to_ref[...] = mm(both[1], jnp.concatenate(twice, axis=1), LEADING)
    lower = lax.broadcasted_iota(jnp.int32, (8, 128), 1) < 64
    for y in range(4):
        for owner in range(2):
            for x in range(4):
                rows = [
                    tq_ref[pl.ds(s * 256 + y * 48 + owner * 24, 24), pl.ds(x * 256, 256)]
                    for s in range(4)
                ]
                for z in range(4):
                    sides = []
                    for upper in range(2):
                        start = (z + upper * 4) * 128 + y * 32 + owner * 16
                        low = to_ref[pl.ds(start, 8), pl.ds(x * 128, 128)]
                        high = to_ref[pl.ds(start + 8, 8), pl.ds(x * 128, 128)]
                        sides.append(jnp.where(lower, low, high))
                    rows.append(jnp.concatenate(sides, axis=1))
                out_ref[y, owner, x] = jnp.concatenate(rows, axis=0).astype(bf16)


def head_parts(got_ref, wo_ref, back):
    lanes = lax.broadcasted_iota(jnp.int32, (CELLS, 256), 1)
    heads = jnp.concatenate([back[:, s * 256 + 192 : s * 256 + 256] for s in range(4)], axis=1)
    total = None
    for s in range(4):
        part = jnp.where(lanes < 192, back[:, s * 256 : s * 256 + 256], 0)
        term = mm(part, got_ref[s], TRAILING)
        total = term if total is None else total + term
    return mm(heads, wo_ref[...]), total


def home_kernel(
    ints_ref, normf_ref, inv_ref, tok_ref, dy_ref, got_ref, wo_ref, back_ref, came_ref,
    out_ref, gtok_ref, east_ref, south_ref, corner_ref,
):
    own, halo = scatter_matrices([ints_ref[k] for k in range(3)])

    def edges(which, values):
        edge = mm(halo, values).astype(bf16)
        east_ref[which] = edge[:EAST]
        south_ref[which] = edge[EAST : 2 * EAST]
        corner_ref[which] = edge[2 * EAST : 2 * EAST + CORNER]

    branch, dnormed = head_parts(got_ref, wo_ref, back_ref[pl.ds(0, CELLS)])
    branch = (branch + came_ref[0].astype(f32)).astype(bf16)
    edges(0, branch)
    out_ref[...] = (tok_ref[...].astype(f32) + mm(own, branch)).astype(bf16)
    dnormed = dnormed + came_ref[1].astype(f32)
    normed_f = normf_ref[...]
    dnorm = inv_ref[:, :1] * (
        dnormed
        - jnp.mean(dnormed, -1, keepdims=True)
        - normed_f * jnp.mean(dnormed * normed_f, -1, keepdims=True)
    )
    high = dnorm.astype(bf16)
    low = (dnorm - high.astype(f32)).astype(bf16)
    edges(1, high)
    gtok_ref[...] = (dy_ref[...].astype(f32) + (mm(own, high) + mm(own, low))).astype(bf16)


def finish_kernel(out_ref, gtok_ref, west_ref, north_ref, corner_ref, out2_ref, gtok2_ref):
    place = arrived_matrix()
    pad = jnp.zeros((128 - 2 * EAST - CORNER, out_ref.shape[1]), bf16)
    for which, (part, result) in enumerate(((out_ref, out2_ref), (gtok_ref, gtok2_ref))):
        edge = jnp.concatenate([west_ref[which], north_ref[which], corner_ref[which], pad], axis=0)
        result[...] = (part[...].astype(f32) + mm(place, edge)).astype(bf16)


def plane_kernel(got_ref, out_ref, total_ref):
    for core in range(2):
        total = None
        for y in range(4):
            for x in range(4):
                part = got_ref[y * 8 + core * 4 + x].astype(f32)
                total = part if total is None else total + part
        total_ref[core] = total
    for z in range(8):
        for half in range(2):
            out_ref[z, half, :24] = total_ref[z % 2, pl.ds(z // 2 * 24, 24), pl.ds(half * 128, 128)]
            out_ref[z, half, 24:] = total_ref[half, pl.ds(96 + z % 4 * 8, 8), pl.ds(z // 4 * 128, 128)]


def last_kernel(got_ref, gq_ref, go_ref):
    total = got_ref[0]
    for part in range(1, 16):
        total = total + got_ref[part]
    gq_ref[...] = total[:24]
    go_ref[...] = jnp.concatenate([total[24:, :64], total[24:, 64:]], axis=0)


def call(kernel, outs, *args, smem=0, scratch=(), flops=0, name=None):
    specs = [pl.BlockSpec(memory_space=pltpu.SMEM)] * smem + [pl.BlockSpec(memory_space=pltpu.VMEM)] * (
        len(args) - smem
    )
    shapes = [jax.ShapeDtypeStruct(s, d) for s, d in outs]
    size = sum(a.size * a.dtype.itemsize for a in (*args, *shapes))
    return pl.pallas_call(
        kernel,
        out_shape=shapes,
        in_specs=specs,
        out_specs=[pl.BlockSpec(memory_space=pltpu.VMEM)] * len(outs),
        scratch_shapes=list(scratch),
        compiler_params=pltpu.CompilerParams(vmem_limit_bytes=VMEM_LIMIT),
        cost_estimate=pl.CostEstimate(flops=flops, bytes_accessed=size, transcendentals=0),
        name=name,
    )(*args)


def position_bias(rel_bias):
    span = 2 * WIN - 1
    places = jnp.arange(WIN * WIN, dtype=jnp.int32)
    row_of = places // WIN
    col_of = places % WIN
    offset = (row_of[None, :] - row_of[:, None] + WIN - 1) * span + (
        col_of[None, :] - col_of[:, None] + WIN - 1
    )
    onehot_table = (
        offset.reshape(-1)[:, None] == jnp.arange(span * span, dtype=jnp.int32)[None, :]
    ).astype(f32)
    picked = jnp.dot(
        onehot_table,
        rel_bias.reshape(HEADS, span * span).T,
        precision=lax.Precision.HIGHEST,
        preferred_element_type=f32,
    )
    table = picked.T.reshape(HEADS, WIN * WIN, WIN * WIN)
    return jnp.concatenate([table, table], axis=2)


TILE_AXES = ("zl", "y", "c")


def shifted(block, distance):
    count = lax.axis_size(TILE_AXES)
    return lax.ppermute(block, TILE_AXES, [((i - distance) % count, i) for i in range(count)])


def per_device(tokens, w_qkv, w_out, rel_bias, seam_codes, corner_open, grad_out):
    width = tokens.shape[-1]
    both = jnp.stack([tokens[0, 0], grad_out[0, 0]])
    tok = tokens.reshape(CELLS, width)
    dy = grad_out.reshape(CELLS, width)
    order = jnp.arange(3, dtype=jnp.int32)
    spot = jnp.where(
        order == 0, lax.axis_index("c"), jnp.where(order == 1, lax.axis_index("zh"), lax.axis_index("y"))
    ).astype(jnp.int32)
    ints = jnp.concatenate([seam_codes[0], corner_open, lax.axis_index("c")[None]]).astype(jnp.int32)

    (piece,) = call(piece_kernel, [((128, 384), bf16)], spot, w_qkv, w_out, smem=1, name="piece")
    across = lax.ppermute(piece, "zh", [(0, 1), (1, 0)])
    bias = position_bias(rel_bias)
    across, both, bias = lax.optimization_barrier((across, both, bias))
    (many,) = call(slots_kernel, [((16, 256, 256), bf16)], spot, piece, across, smem=1, name="slots")
    mine = lax.all_to_all(many, ("y", "x"), 0, 0, tiled=True).reshape(4, width, 256)

    def swapped(block):
        return lax.ppermute(block, "c", [(0, 1), (1, 0)])

    east = shifted(both[:, HALF:, :HALF].reshape(2, EAST, width), -1)
    south = shifted(both[:, :HALF, HALF:].reshape(2, EAST, width), -GRID_COLS)
    corner = shifted(both[:, :HALF, :HALF].reshape(2, CORNER, width), -(GRID_COLS + 1))
    sides, normed_f, inverse = call(
        prep_kernel,
        [((2, CELLS + FLAG_ROWS, width), bf16), ((CELLS, width), f32), ((CELLS, 128), f32)],
        ints, tok, dy, east, south, corner,
        smem=1, flops=4 * 256 * 384 * 1024, name="prep",
    )
    peer = swapped(sides)
    mine, sides, peer = lax.optimization_barrier((mine, sides, peer))
    back, wo, send = call(
        attend_kernel,
        [((2 * CELLS, width), bf16), ((256, width), bf16), ((2, CELLS, width), bf16)],
        ints, sides, peer, mine, bias,
        smem=1, scratch=[pltpu.VMEM((2 * CELLS, 1024), bf16), pltpu.VMEM((2 * CELLS, 256), bf16)],
        flops=2 * 256 * 1024 * 2048, name="attend",
    )
    (pair,) = call(
        grads_kernel,
        [((4, 2, 4, 128, 256), bf16)],
        sides, peer, back,
        scratch=[pltpu.VMEM((1024, 1024), f32), pltpu.VMEM((1024, 512), f32)],
        flops=2 * 512 * 1024 * 1536, name="weight_grads",
    )
    came = swapped(send)
    out_part, gtok_part, east, south, corner = call(
        home_kernel,
        [
            ((CELLS, width), bf16), ((CELLS, width), bf16),
            ((2, EAST, width), bf16), ((2, EAST, width), bf16), ((2, CORNER, width), bf16),
        ],
        ints, normed_f, inverse, tok, dy, mine, wo, back, came, smem=1, flops=2 * 256 * 1024 * 900, name="home",
    )
    north = shifted(south, GRID_COLS)
    corner = shifted(corner, GRID_COLS + 1)
    west = shifted(east, 1)
    plane = lax.all_to_all(pair.reshape(32, 128, 256), ("y", "c", "x"), 0, 0, tiled=True)
    (plane,) = call(
        plane_kernel, [((8, 2, 32, 128), f32)], plane, scratch=[pltpu.VMEM((2, 128, 256), f32)], name="plane_sum"
    )
    plane, west, north, corner = lax.optimization_barrier((plane, west, north, corner))
    column = lax.all_to_all(plane.reshape(16, 32, 128), ("zl", "zh"), 0, 0, tiled=True)
    grad_w_qkv, grad_w_out = call(
        last_kernel, [((24, 128), f32), ((16, 64), f32)], column, name="column_sum"
    )
    output, grad_tokens = call(
        finish_kernel, [((CELLS, width), bf16), ((CELLS, width), bf16)],
        out_part, gtok_part, west, north, corner, name="finish",
    )
    return (
        output.reshape(tokens.shape), grad_tokens.reshape(tokens.shape), grad_w_qkv.T, grad_w_out.T
    )


def solution(mesh):
    fine = Mesh(mesh.devices.reshape(8, 4, 2, 4, 2), ("zl", "y", "c", "x", "zh"))
    fsdp = ("x", "zh")
    acts = P(fsdp, TILE_AXES, None, None, None)
    return jax.shard_map(
        per_device,
        mesh=fine,
        in_specs=(
            acts, P(fsdp, None), P(fsdp, None), P(), P(TILE_AXES, None), P(TILE_AXES), acts,
        ),
        out_specs=(acts, acts, P(fsdp, TILE_AXES), P(fsdp, TILE_AXES)),
        check_vma=False,
    )
```

```python
import functools
import jax
import jax.numpy as jnp
from jax import lax
from jax.experimental import pallas as pl
from jax.experimental.pallas import tpu as pltpu
from jax.sharding import Mesh, PartitionSpec as P

HEADS = 8
HD = 64
WIN = 8
GRID_COLS = 8
SIDE = 16
HALF = WIN // 2
INNER = SIDE - HALF
CELLS = SIDE * SIDE
FLAG_ROWS = 16
EAST = INNER * HALF
CORNER = HALF * HALF
EPSILON = 1e-05
NEG = -1e30
TRAILING = (((1,), (1,)), ((), ()))
LEADING = (((0,), (0,)), ((), ()))
VMEM_LIMIT = 56 * 1024 * 1024

f32 = jnp.float32
bf16 = jnp.bfloat16


def mm(a, b, dims=(((1,), (0,)), ((), ()))):
    return lax.dot_general(a, b, dims, preferred_element_type=f32)


def region_coords(shape, axis):
    place = lax.broadcasted_iota(jnp.int32, shape, axis)
    window, inside = place >> 6, place & 63
    row = (window >> 1) * WIN + (inside >> 3)
    column = (window & 1) * WIN + (inside & 7)
    return row, column


def source_of(codes, shape, axis):
    row, column = region_coords(shape, axis)
    flip_one, flip_two = codes[0] & 1, codes[0] >> 1
    er = jnp.where(flip_one == 1, INNER - 1 - row, row)
    ec = column - INNER
    ec = jnp.where(flip_two == 1, HALF - 1 - ec, ec)
    flip_one, flip_two = codes[1] & 1, codes[1] >> 1
    sc = jnp.where(flip_one == 1, INNER - 1 - column, column)
    sr = row - INNER
    sr = jnp.where(flip_two == 1, HALF - 1 - sr, sr)
    i, j = row - INNER, column - INNER
    turn = codes[2]
    last = HALF - 1
    cr = jnp.where(turn == 0, i, jnp.where(turn == 1, j, jnp.where(turn == 2, last - i, last - j)))
    cc = jnp.where(turn == 0, j, jnp.where(turn == 1, last - i, jnp.where(turn == 2, last - j, i)))
    own = (row + HALF) * SIDE + column + HALF
    east = CELLS + er * HALF + ec
    south = CELLS + EAST + sr * INNER + sc
    corner = CELLS + 2 * EAST + cr * HALF + cc
    low_row, low_column = row < INNER, column < INNER
    return jnp.where(
        low_row, jnp.where(low_column, own, east), jnp.where(low_column, south, corner)
    )


def onehot(condition):
    return jnp.where(condition, 1.0, 0.0).astype(bf16)


def gather_matrices(codes):
    source = source_of(codes, (CELLS, 1), 0)
    own = onehot(source == lax.broadcasted_iota(jnp.int32, (CELLS, CELLS), 1))
    halo = onehot(source - CELLS == lax.broadcasted_iota(jnp.int32, (CELLS, 128), 1))
    return own, halo


def scatter_matrices(codes):
    source = source_of(codes, (1, CELLS), 1)
    own = onehot(source == lax.broadcasted_iota(jnp.int32, (CELLS, CELLS), 0))
    halo = onehot(source - CELLS == lax.broadcasted_iota(jnp.int32, (128, CELLS), 0))
    return own, halo


def arrived_matrix():
    place = lax.broadcasted_iota(jnp.int32, (CELLS, 1), 0)
    row, column = place >> 4, place & 15
    west = (row - HALF) * HALF + column
    north = EAST + row * INNER + column - HALF
    corner = 2 * EAST + row * HALF + column
    low_row, low_column = row < HALF, column < HALF
    index = jnp.where(
        low_row,
        jnp.where(low_column, corner, north),
        jnp.where(low_column, west, -1),
    )
    return onehot(index == lax.broadcasted_iota(jnp.int32, (CELLS, 128), 1))


def prep_kernel(ints_ref, tok_ref, dy_ref, e_ref, s_ref, c_ref, sides_ref, normf_ref, inv_ref):
    codes = [ints_ref[k] for k in range(3)]
    own, halo = gather_matrices(codes)
    pad = jnp.zeros((128 - 2 * EAST - CORNER, tok_ref.shape[1]), bf16)

    def region(main, which):
        edge = jnp.concatenate([e_ref[which], s_ref[which], c_ref[which], pad], axis=0)
        return mm(own, main) + mm(halo, edge)

    values = region(tok_ref[...], 0)
    center = values - jnp.mean(values, -1, keepdims=True)
    variance = jnp.mean(center * center, -1, keepdims=True)
    inverse = lax.rsqrt(variance + EPSILON)
    normed_f = center * inverse
    normf_ref[...] = normed_f
    sides_ref[0, :CELLS] = normed_f.astype(bf16)
    flag = jnp.where(ints_ref[3] == 0, 0.0, 1.0)
    sides_ref[0, CELLS:] = jnp.full((FLAG_ROWS, tok_ref.shape[1]), flag, f32).astype(bf16)
    sides_ref[1, CELLS:] = jnp.zeros((FLAG_ROWS, tok_ref.shape[1]), bf16)
    inv_ref[...] = jnp.broadcast_to(inverse, inv_ref.shape)
    sides_ref[1, :CELLS] = region(dy_ref[...], 1).astype(bf16)


def piece_kernel(spot_ref, wq_ref, wo_ref, out_ref):
    core, y = spot_ref[0], spot_ref[2]
    wq, wo = wq_ref[...], wo_ref[...]
    head = y * 2 + core
    part = wq[:, :192]
    for k in range(1, HEADS):
        part = jnp.where(head == k, wq[:, k * 192 : (k + 1) * 192], part)
    quarter = wo[:, :256]
    for k in range(1, 4):
        quarter = jnp.where(y == k, wo[:, k * 256 : (k + 1) * 256], quarter)
    group = [quarter[:, k * 64 : (k + 1) * 64] for k in range(4)]
    low = jnp.concatenate([group[0], group[2]], axis=1)
    high = jnp.concatenate([group[1], group[3]], axis=1)
    out_ref[...] = jnp.concatenate(
        [part, jnp.zeros((128, 64), bf16), jnp.concatenate([low, high], axis=0)], axis=1
    )


def slots_kernel(spot_ref, here_ref, there_ref, out_ref):
    core, zh = spot_ref[0], spot_ref[1]
    here, there = here_ref[...], there_ref[...]
    first = jnp.where(zh == 0, here, there)
    second = jnp.where(zh == 0, there, here)
    out = jnp.where(core == zh, here, there)[:, 256:]
    slot = jnp.concatenate(
        [
            jnp.concatenate([first[:, :192], out[:, :64]], axis=1),
            jnp.concatenate([second[:, :192], out[:, 64:]], axis=1),
        ],
        axis=0,
    )
    for k in range(16):
        out_ref[k] = slot


def attend_kernel(
    ints_ref, sides_ref, peer_hbm, got_ref, bias_ref, back_ref, wo_ref, send_ref,
    qkv_ref, gh_ref, peer_ref, sem,
):
    core = ints_ref[4]
    copy = pltpu.make_async_copy(peer_hbm, peer_ref, sem)
    copy.start()
    for s in range(4):
        qkv_ref[pl.ds(0, CELLS), pl.ds(s * 256, 256)] = mm(sides_ref[0, :CELLS], got_ref[s]).astype(bf16)
        for y in range(4):
            row = [got_ref[y, pl.ds(s * 256 + q * 64, 64), pl.ds(128, 128)][:, 64:] for q in range(4)]
            wo_ref[pl.ds(s * 64, 64), pl.ds(y * 256, 256)] = jnp.concatenate(row, axis=1)
    gh_ref[pl.ds(0, CELLS)] = mm(sides_ref[1, :CELLS], wo_ref[...], TRAILING).astype(bf16)
    copy.wait()
    for s in range(4):
        qkv_ref[pl.ds(CELLS, CELLS), pl.ds(s * 256, 256)] = mm(peer_ref[0, :CELLS], got_ref[s]).astype(bf16)
    gh_ref[pl.ds(CELLS, CELLS)] = mm(peer_ref[1, :CELLS], wo_ref[...], TRAILING).astype(bf16)
    keys = lax.broadcasted_iota(jnp.int32, (128, 128), 0)
    lower = lax.broadcasted_iota(jnp.int32, (64, 128), 1) < 64
    query = lax.broadcasted_iota(jnp.int32, (1, 128), 1)

    def closed(place):
        inside = place & 63
        return (place >= 64) & ((inside >> 3) >= HALF) & ((inside & 7) >= HALF)

    no_key, keep = [], []
    for ref in (sides_ref, peer_ref):
        flag = ref[0, CELLS:, :128].astype(f32)[:1]
        no_key.append(jnp.where(closed(keys) & (flag == 0.0), NEG, 0.0))
        keep.append(jnp.where(closed(query) & (flag == 0.0), 0.0, 1.0))
    scale = jnp.asarray(HD ** (-0.5), bf16)
    n = range(4)
    for head in range(4):
        table = bias_ref[head * 2 + core]
        table = jnp.concatenate([jnp.where(lower, table, NEG), jnp.where(lower, NEG, table)], axis=0)
        q, k, v, g = [], [], [], []
        for block in n:
            wide = qkv_ref[pl.ds(block * 128, 128), pl.ds(head * 256, 256)]
            q.append(wide[:, :64] * scale)
            k.append(wide[:, 64:128])
            v.append(wide[:, 128:192])
            pair = gh_ref[pl.ds(block * 128, 128), pl.ds(head // 2 * 128, 128)]
            g.append(pair[:, head % 2 * 64 : head % 2 * 64 + 64])
        score = [mm(k[u], q[u], TRAILING) + table for u in n]
        score = [score[u] + no_key[u // 2] if u % 2 == 1 else score[u] for u in n]
        dp = [mm(v[u], g[u], TRAILING) for u in n]
        e = [jnp.exp(score[u] - jnp.max(score[u], 0, keepdims=True)) for u in n]
        r = [1.0 / jnp.sum(e[u], 0, keepdims=True) for u in n]
        r = [r[u] * keep[u // 2] if u % 2 == 1 else r[u] for u in n]
        probs = [e[u] * r[u] for u in n]
        pb = [probs[u].astype(bf16) for u in n]
        ds = [
            (probs[u] * (dp[u] - jnp.sum(dp[u] * probs[u], 0, keepdims=True))).astype(bf16) for u in n
        ]
        out = [mm(pb[u], v[u], LEADING).astype(bf16) for u in n]
        dv = [mm(pb[u], g[u]).astype(bf16) for u in n]
        dq = [mm(ds[u], k[u] * scale, LEADING).astype(bf16) for u in n]
        dk = [mm(ds[u], q[u]).astype(bf16) for u in n]
        for u in n:
            back_ref[pl.ds(u * 128, 128), pl.ds(head * 256, 256)] = jnp.concatenate(
                [dq[u], dk[u], dv[u], out[u]], axis=1
            )
    branch, dnormed = head_parts(got_ref, wo_ref, back_ref[pl.ds(CELLS, CELLS)])
    send_ref[0] = branch.astype(bf16)
    send_ref[1] = dnormed.astype(bf16)


def grads_kernel(sides_ref, peer_ref, back_ref, out_ref, tq_ref, to_ref):
    both = [jnp.concatenate([sides_ref[k, :CELLS], peer_ref[k, :CELLS]], axis=0) for k in range(2)]
    back = back_ref[...]
    tq_ref[...] = mm(back, both[0], LEADING)
    twice = []
    for head in range(4):
        one = back[:, head * 256 + 192 : head * 256 + 256]
        twice += [one, one]
    to_ref[...] = mm(both[1], jnp.concatenate(twice, axis=1), LEADING)
    lower = lax.broadcasted_iota(jnp.int32, (8, 128), 1) < 64
    for y in range(4):
        for owner in range(2):
            for x in range(4):
                rows = [
                    tq_ref[pl.ds(s * 256 + y * 48 + owner * 24, 24), pl.ds(x * 256, 256)]
                    for s in range(4)
                ]
                for z in range(4):
                    sides = []
                    for upper in range(2):
                        start = (z + upper * 4) * 128 + y * 32 + owner * 16
                        low = to_ref[pl.ds(start, 8), pl.ds(x * 128, 128)]
                        high = to_ref[pl.ds(start + 8, 8), pl.ds(x * 128, 128)]
                        sides.append(jnp.where(lower, low, high))
                    rows.append(jnp.concatenate(sides, axis=1))
                out_ref[y, owner, x] = jnp.concatenate(rows, axis=0).astype(bf16)


def head_parts(got_ref, wo_ref, back):
    lanes = lax.broadcasted_iota(jnp.int32, (CELLS, 256), 1)
    heads = jnp.concatenate([back[:, s * 256 + 192 : s * 256 + 256] for s in range(4)], axis=1)
    total = None
    for s in range(4):
        part = jnp.where(lanes < 192, back[:, s * 256 : s * 256 + 256], 0)
        term = mm(part, got_ref[s], TRAILING)
        total = term if total is None else total + term
    return mm(heads, wo_ref[...]), total


def home_kernel(
    ints_ref, normf_ref, inv_ref, tok_ref, dy_ref, got_ref, wo_ref, back_ref, came_hbm,
    out_ref, gtok_ref, east_ref, south_ref, corner_ref, came_ref, sem,
):
    copy = pltpu.make_async_copy(came_hbm, came_ref, sem)
    copy.start()
    own, halo = scatter_matrices([ints_ref[k] for k in range(3)])

    def edges(which, values):
        edge = mm(halo, values).astype(bf16)
        east_ref[which] = edge[:EAST]
        south_ref[which] = edge[EAST : 2 * EAST]
        corner_ref[which] = edge[2 * EAST : 2 * EAST + CORNER]

    branch, dnormed = head_parts(got_ref, wo_ref, back_ref[pl.ds(0, CELLS)])
    copy.wait()
    branch = (branch + came_ref[0].astype(f32)).astype(bf16)
    edges(0, branch)
    out_ref[...] = (tok_ref[...].astype(f32) + mm(own, branch)).astype(bf16)
    dnormed = dnormed + came_ref[1].astype(f32)
    normed_f = normf_ref[...]
    dnorm = inv_ref[:, :1] * (
        dnormed
        - jnp.mean(dnormed, -1, keepdims=True)
        - normed_f * jnp.mean(dnormed * normed_f, -1, keepdims=True)
    )
    high = dnorm.astype(bf16)
    low = (dnorm - high.astype(f32)).astype(bf16)
    edges(1, high)
    gtok_ref[...] = (dy_ref[...].astype(f32) + (mm(own, high) + mm(own, low))).astype(bf16)


def finish_kernel(out_ref, gtok_ref, west_ref, north_ref, corner_ref, out2_ref, gtok2_ref):
    place = arrived_matrix()
    pad = jnp.zeros((128 - 2 * EAST - CORNER, out_ref.shape[1]), bf16)
    for which, (part, result) in enumerate(((out_ref, out2_ref), (gtok_ref, gtok2_ref))):
        edge = jnp.concatenate([west_ref[which], north_ref[which], corner_ref[which], pad], axis=0)
        result[...] = (part[...].astype(f32) + mm(place, edge)).astype(bf16)


def plane_kernel(got_ref, out_ref, total_ref):
    for core in range(2):
        total = None
        for y in range(4):
            for x in range(4):
                part = got_ref[y * 8 + core * 4 + x].astype(f32)
                total = part if total is None else total + part
        total_ref[core] = total
    for z in range(8):
        for half in range(2):
            out_ref[z, half, :24] = total_ref[z % 2, pl.ds(z // 2 * 24, 24), pl.ds(half * 128, 128)]
            out_ref[z, half, 24:] = total_ref[half, pl.ds(96 + z % 4 * 8, 8), pl.ds(z // 4 * 128, 128)]


def last_kernel(got_ref, gq_ref, go_ref):
    total = got_ref[0]
    for part in range(1, 16):
        total = total + got_ref[part]
    gq_ref[...] = total[:24]
    go_ref[...] = jnp.concatenate([total[24:, :64], total[24:, 64:]], axis=0)


def call(kernel, outs, *args, smem=0, hbm=(), scratch=(), flops=0, name=None):
    specs = [pl.BlockSpec(memory_space=pltpu.SMEM)] * smem + [pl.BlockSpec(memory_space=pltpu.VMEM)] * (
        len(args) - smem
    )
    for k in hbm:
        specs[k] = pl.BlockSpec(memory_space=pl.ANY)
    shapes = [jax.ShapeDtypeStruct(s, d) for s, d in outs]
    size = sum(a.size * a.dtype.itemsize for a in (*args, *shapes))
    return pl.pallas_call(
        kernel,
        out_shape=shapes,
        in_specs=specs,
        out_specs=[pl.BlockSpec(memory_space=pltpu.VMEM)] * len(outs),
        scratch_shapes=list(scratch),
        compiler_params=pltpu.CompilerParams(vmem_limit_bytes=60 * 2**20 if hbm else VMEM_LIMIT),
        cost_estimate=pl.CostEstimate(flops=flops, bytes_accessed=size, transcendentals=0),
        name=name,
    )(*args)


def position_bias(rel_bias):
    span = 2 * WIN - 1
    places = jnp.arange(WIN * WIN, dtype=jnp.int32)
    row_of = places // WIN
    col_of = places % WIN
    offset = (row_of[None, :] - row_of[:, None] + WIN - 1) * span + (
        col_of[None, :] - col_of[:, None] + WIN - 1
    )
    onehot_table = (
        offset.reshape(-1)[:, None] == jnp.arange(span * span, dtype=jnp.int32)[None, :]
    ).astype(f32)
    picked = jnp.dot(
        onehot_table,
        rel_bias.reshape(HEADS, span * span).T,
        precision=lax.Precision.HIGHEST,
        preferred_element_type=f32,
    )
    table = picked.T.reshape(HEADS, WIN * WIN, WIN * WIN)
    return jnp.concatenate([table, table], axis=2)


TILE_AXES = ("zl", "y", "c")


def shifted(block, distance):
    count = lax.axis_size(TILE_AXES)
    return lax.ppermute(block, TILE_AXES, [((i - distance) % count, i) for i in range(count)])


def per_device(tokens, w_qkv, w_out, rel_bias, seam_codes, corner_open, grad_out):
    width = tokens.shape[-1]
    both = jnp.stack([tokens[0, 0], grad_out[0, 0]])
    tok = tokens.reshape(CELLS, width)
    dy = grad_out.reshape(CELLS, width)
    order = jnp.arange(3, dtype=jnp.int32)
    spot = jnp.where(
        order == 0, lax.axis_index("c"), jnp.where(order == 1, lax.axis_index("zh"), lax.axis_index("y"))
    ).astype(jnp.int32)
    ints = jnp.concatenate([seam_codes[0], corner_open, lax.axis_index("c")[None]]).astype(jnp.int32)

    (piece,) = call(piece_kernel, [((128, 384), bf16)], spot, w_qkv, w_out, smem=1, name="piece")
    across = lax.ppermute(piece, "zh", [(0, 1), (1, 0)])
    bias = position_bias(rel_bias)
    across, both, bias = lax.optimization_barrier((across, both, bias))
    (many,) = call(slots_kernel, [((16, 256, 256), bf16)], spot, piece, across, smem=1, name="slots")
    mine = lax.all_to_all(many, ("y", "x"), 0, 0, tiled=True).reshape(4, width, 256)

    def swapped(block):
        return lax.ppermute(block, "c", [(0, 1), (1, 0)])

    east = shifted(both[:, HALF:, :HALF].reshape(2, EAST, width), -1)
    south = shifted(both[:, :HALF, HALF:].reshape(2, EAST, width), -GRID_COLS)
    corner = shifted(both[:, :HALF, :HALF].reshape(2, CORNER, width), -(GRID_COLS + 1))
    sides, normed_f, inverse = call(
        prep_kernel,
        [((2, CELLS + FLAG_ROWS, width), bf16), ((CELLS, width), f32), ((CELLS, 128), f32)],
        ints, tok, dy, east, south, corner,
        smem=1, flops=4 * 256 * 384 * 1024, name="prep",
    )
    peer = swapped(sides)
    mine, sides, peer = lax.optimization_barrier((mine, sides, peer))
    back, wo, send = call(
        attend_kernel,
        [((2 * CELLS, width), bf16), ((256, width), bf16), ((2, CELLS, width), bf16)],
        ints, sides, peer, mine, bias,
        smem=1, hbm=(2,), scratch=[
            pltpu.VMEM((2 * CELLS, 1024), bf16), pltpu.VMEM((2 * CELLS, 256), bf16),
            pltpu.VMEM((2, CELLS + FLAG_ROWS, 1024), bf16), pltpu.SemaphoreType.DMA,
        ],
        flops=2 * 256 * 1024 * 2048, name="attend",
    )
    (pair,) = call(
        grads_kernel,
        [((4, 2, 4, 128, 256), bf16)],
        sides, peer, back,
        scratch=[pltpu.VMEM((1024, 1024), f32), pltpu.VMEM((1024, 512), f32)],
        flops=2 * 512 * 1024 * 1536, name="weight_grads",
    )
    came = swapped(send)
    out_part, gtok_part, east, south, corner = call(
        home_kernel,
        [
            ((CELLS, width), bf16), ((CELLS, width), bf16),
            ((2, EAST, width), bf16), ((2, EAST, width), bf16), ((2, CORNER, width), bf16),
        ],
        ints, normed_f, inverse, tok, dy, mine, wo, back, came, smem=1, hbm=(8,),
        scratch=[pltpu.VMEM((2, CELLS, width), bf16), pltpu.SemaphoreType.DMA], flops=2 * 256 * 1024 * 900, name="home",
    )
    north = shifted(south, GRID_COLS)
    corner = shifted(corner, GRID_COLS + 1)
    west = shifted(east, 1)
    plane = lax.all_to_all(pair.reshape(32, 128, 256), ("y", "c", "x"), 0, 0, tiled=True)
    (plane,) = call(
        plane_kernel, [((8, 2, 32, 128), f32)], plane, scratch=[pltpu.VMEM((2, 128, 256), f32)], name="plane_sum"
    )
    plane, west, north, corner = lax.optimization_barrier((plane, west, north, corner))
    column = lax.all_to_all(plane.reshape(16, 32, 128), ("zl", "zh"), 0, 0, tiled=True)
    grad_w_qkv, grad_w_out = call(
        last_kernel, [((24, 128), f32), ((16, 64), f32)], column, name="column_sum"
    )
    output, grad_tokens = call(
        finish_kernel, [((CELLS, width), bf16), ((CELLS, width), bf16)],
        out_part, gtok_part, west, north, corner, name="finish",
    )
    return (
        output.reshape(tokens.shape), grad_tokens.reshape(tokens.shape), grad_w_qkv.T, grad_w_out.T
    )


def solution(mesh):
    fine = Mesh(mesh.devices.reshape(8, 4, 2, 4, 2), ("zl", "y", "c", "x", "zh"))
    fsdp = ("x", "zh")
    acts = P(fsdp, TILE_AXES, None, None, None)
    return jax.shard_map(
        per_device,
        mesh=fine,
        in_specs=(
            acts, P(fsdp, None), P(fsdp, None), P(), P(TILE_AXES, None), P(TILE_AXES), acts,
        ),
        out_specs=(acts, acts, P(fsdp, TILE_AXES), P(fsdp, TILE_AXES)),
        check_vma=False,
    )
```
